32 devices in a mesh: wide: 8 (over z, x), narrow: 4 (over y, core).
Axes of the slice: x: 2, y: 2, z: 4, core: 2. Of those that a mesh axis runs over, the one named last changes fastest.
Arguments:
- frames: bfloat16 [8, 512, 1024], P('wide', 'narrow'), may hold values from -6 to 6
- out_grad: bfloat16 [8, 512, 1024], P('wide', 'narrow'), may hold values from -6 to 6
- qkv_weight: bfloat16 [1024, 3072], P(('wide', 'narrow')), may hold values from -0.1875 to 0.1875
- out_weight: bfloat16 [1024, 1024], P(('wide', 'narrow')), may hold values from -0.75 to 0.75
- gate_up_weight: bfloat16 [1024, 8192], P(('wide', 'narrow')), may hold values from -0.1875 to 0.1875
- down_weight_t: bfloat16 [1024, 4096], P(('wide', 'narrow')), may hold values from -0.09375 to 0.09375
- norm_gain_one: float32 [1024], replicated, may hold values from 0.5 to 1.5
- norm_gain_two: float32 [1024], replicated, may hold values from 0.5 to 1.5
- layer_scale_one: float32 [1024], replicated, may hold values from 0.5 to 1.5
- layer_scale_two: float32 [1024], replicated, may hold values from 0.5 to 1.5
- speaker: int32 [8], P('wide'), may hold values from 0 to 127
- clip_bounds: int32 [8, 2], P('wide'), may hold values from 1 to 512, as said below
Outputs:
- output: bfloat16 [8, 512, 1024], P('wide', 'narrow')
- speaker_power: float32 [128, 1024], replicated
- frames_grad: bfloat16 [8, 512, 1024], P('wide', 'narrow')
- qkv_weight_grad: float32 [1024, 3072], P('wide', 'narrow')
- out_weight_grad: float32 [1024, 1024], P('wide', 'narrow')
- gate_up_weight_grad: float32 [1024, 8192], P('wide', 'narrow')
- down_weight_grad: float32 [1024, 4096], P('wide', 'narrow')
- norm_gain_one_grad: float32 [1024], replicated
- norm_gain_two_grad: float32 [1024], replicated
- layer_scale_one_grad: float32 [1024], replicated
- layer_scale_two_grad: float32 [1024], replicated
The draws below stay inside these ranges and needn't reach their ends.
Inputs may be any that keep to these rules, and one draw needn't show every extreme that they name: Each stream holds at most three clips; clip_bounds[s, 0] < clip_bounds[s, 1] (a third clip is empty when its start is 512). In each block of 1 streams, one stream drawn from the seed has its second clip start before frame 128 and its third after frame 512 - 128; in the first block that stream's bounds are 1 and 512.
All inputs are finite; a program needn't handle non-finite values.
Results may differ from the reference program's by a relative error of at most 0.015.
Values may be sent and summed in bfloat16 or wider, within the bound.
No kernel may reach another device: no remote copies, remote signals or barrier semaphores. Data moves between devices by JAX's collectives and lax.ppermute only.
A program may use at most 192 MiB of HBM per device.

```python
import math
import jax
import jax.numpy as jnp
from jax import lax

D = 1024
HEADS = 16
HEAD = 64
FF = 4096
WINDOW = 128
CLIP_LEN = 512
STREAMS_DEV = 1
SPEAKERS = 128
SHARD = 128
STREAMS = 8


def draw_clip_bounds(key, part):
    key = jax.random.fold_in(key, 7)
    cut_keys = jax.random.split(key, 5)
    first_cut = jax.random.randint(cut_keys[0], (STREAMS,), 1, CLIP_LEN - 1)
    second_cut = jax.random.randint(cut_keys[1], (STREAMS,), first_cut + 1, CLIP_LEN + 1)
    long_first = jax.random.randint(cut_keys[2], (STREAMS,), 1, SHARD)
    long_second = jax.random.randint(cut_keys[3], (STREAMS,), CLIP_LEN - SHARD + 1, CLIP_LEN + 1)
    chosen = jax.random.randint(cut_keys[4], (STREAMS // STREAMS_DEV,), 0, STREAMS_DEV)
    stream_index = jnp.arange(STREAMS)
    is_long = stream_index % STREAMS_DEV == jnp.repeat(chosen, STREAMS_DEV, total_repeat_length=STREAMS)
    first_block = stream_index < STREAMS_DEV
    long_first = jnp.where(first_block, 1, long_first)
    long_second = jnp.where(first_block, CLIP_LEN, long_second)
    lower_cut = jnp.where(is_long, long_first, first_cut)
    upper_cut = jnp.where(is_long, long_second, second_cut)
    return jnp.stack([lower_cut, upper_cut], axis=1).astype(jnp.int32)


def plant(values, rng, smallest, largest):
    longest = values.shape.index(max(values.shape))
    spots = []
    for shift in (0, 1):
        where = [jax.random.randint(jax.random.fold_in(rng, axis), (), 0, length) for axis, length in enumerate(values.shape)]
        where[longest] = (where[longest] + shift) % values.shape[longest]
        spots.append(tuple(where))
    return values.at[spots[0]].set(smallest).at[spots[1]].set(largest)


def steps_of(own_key, dims, shards, smallest, largest):
    factor_of = 1.0
    for dim, parts in shards:
        draws = jax.random.uniform(jax.random.fold_in(jax.random.fold_in(own_key, 6), dim), (parts,), jnp.float32, smallest / len(shards), largest / len(shards))
        factor_of = factor_of * jnp.repeat(jnp.exp(draws), dims[dim] // parts).reshape((-1,) + (1,) * (len(dims) - 1 - dim))
    return factor_of


def normal_values(key, dims, deviation, reach, cuts=(), kind=jnp.bfloat16):
    values = jax.random.normal(key, dims, jnp.float32) * deviation
    if len(cuts) > 0:
        values = steps_of(key, dims, cuts, -0.22, 0.18) * values
    return jnp.clip(values, min=-reach, max=reach).astype(kind)


def setup_inputs(seed: int = 0) -> dict:
    streams_of = jax.random.split(jax.random.key(seed), 13)
    frames = normal_values(streams_of[0], (STREAMS, CLIP_LEN, D), 1.0, 6.0, ((0, 8), (1, 4)))
    out_grad = normal_values(streams_of[1], (STREAMS, CLIP_LEN, D), 1.0, 6.0, ((0, 8), (1, 4)))
    qkv_weight = normal_values(streams_of[2], (D, 3 * D), D ** -0.5, 0.1875, ((0, 32),))
    out_weight = normal_values(streams_of[3], (D, D), (D // 16) ** -0.5, 0.75, ((0, 32),))
    gate_up_weight = normal_values(streams_of[4], (D, 2 * FF), D ** -0.5, 0.1875, ((0, 32),))
    down_weight_t = normal_values(streams_of[5], (D, FF), FF ** -0.5, 0.09375, ((0, 32),))
    norm_gain_one = jnp.clip(1.0 + 0.1 * jax.random.normal(streams_of[6], (D,), jnp.float32), 0.5, 1.5)
    norm_gain_two = jnp.clip(1.0 + 0.1 * jax.random.normal(streams_of[7], (D,), jnp.float32), 0.5, 1.5)
    layer_scale_one = jnp.clip(jnp.exp(jax.random.uniform(streams_of[8], (D,), jnp.float32, math.log(0.5), math.log(1.5))), 0.5, 1.5)
    layer_scale_two = jnp.clip(jnp.exp(jax.random.uniform(streams_of[9], (D,), jnp.float32, math.log(0.5), math.log(1.5))), 0.5, 1.5)
    speaker = plant(jax.random.randint(streams_of[10], (STREAMS,), 0, SPEAKERS), jax.random.fold_in(streams_of[10], 1), 0, SPEAKERS - 1).astype(jnp.int32)
    clip_bounds = draw_clip_bounds(jax.random.fold_in(streams_of[12], 71), 0)
    return dict(frames=frames, out_grad=out_grad, qkv_weight=qkv_weight, out_weight=out_weight, gate_up_weight=gate_up_weight, down_weight_t=down_weight_t, norm_gain_one=norm_gain_one, norm_gain_two=norm_gain_two, layer_scale_one=layer_scale_one, layer_scale_two=layer_scale_two, speaker=speaker, clip_bounds=clip_bounds)


highest = lax.Precision.HIGHEST

@jax.custom_vjp
def low(v):
    return lax.optimization_barrier(v.astype(jnp.bfloat16)).astype(jnp.float32)

@jax.custom_vjp
def low_back(v):
    return v

def low_keep(v):
    return (low(v), None)

def low_pass(kept, grad):
    return (grad,)

def back_keep(v):
    return (v, None)

def back_low(kept, grad):
    return (low(grad),)
low.defvjp(low_keep, low_pass)
low_back.defvjp(back_keep, back_low)

def rotary_tables(positions, head_size):
    half_size = head_size // 2
    inverse_freq = jnp.exp(jnp.arange(half_size, dtype=jnp.float32) * (-math.log(10000.0) / half_size))
    angles = positions[:, None] * inverse_freq[None, :]
    return (jnp.cos(angles)[:, None, :], jnp.sin(angles)[:, None, :])

def rotate(vector, cosine, sine_table):
    half_size = vector.shape[-1] // 2
    lower = vector[..., :half_size]
    upper = vector[..., half_size:]
    return jnp.concatenate([lower * cosine - upper * sine_table, upper * cosine + lower * sine_table], axis=-1)

def clip_segments(positions, clip_bounds):
    return (positions[None, :] >= clip_bounds[:, 0:1]).astype(jnp.int32) + (positions[None, :] >= clip_bounds[:, 1:2]).astype(jnp.int32)

def layer_norm(values, norm_gain):
    centred = values - lax.optimization_barrier(jnp.mean(values, axis=-1, keepdims=True))
    spread = lax.optimization_barrier(jnp.mean(centred * centred, axis=-1, keepdims=True))
    return centred * lax.rsqrt(spread + 1e-05) * norm_gain

def block_forward(tokens, qkv_weight, out_weight, gate_up_weight, down_weight_t, norm_gain_one, norm_gain_two, layer_scale_one, layer_scale_two, clip_bounds):
    groups_here = tokens.shape[0]
    positions = jnp.arange(CLIP_LEN, dtype=jnp.int32)
    cosine, sine_table = rotary_tables(positions.astype(jnp.float32), HEAD)
    normed_one = low(layer_norm(tokens, norm_gain_one))
    projected = low_back(jnp.einsum('gtd,de->gte', normed_one, qkv_weight, precision=highest))
    head_shape = (groups_here, CLIP_LEN, HEADS, HEAD)
    queries = low(rotate(projected[..., :D].reshape(head_shape), cosine, sine_table))
    key_rot = low(rotate(projected[..., D:2 * D].reshape(head_shape), cosine, sine_table))
    value_part = low(projected[..., 2 * D:].reshape(head_shape))
    segments = clip_segments(positions, clip_bounds)
    near = jnp.abs(positions[:, None] - positions[None, :]) <= WINDOW
    allowed = near[None, None] & (segments[:, :, None] == segments[:, None, :])[:, None]
    scores = low_back(jnp.einsum('gqhe,gkhe->ghqk', queries, key_rot, precision=highest) * HEAD ** (-0.5))
    attn_weights = low(jax.nn.softmax(jnp.where(allowed, scores, -1e+30), axis=-1))
    attended = low_back(low(jnp.einsum('ghqk,gkhe->gqhe', attn_weights, value_part, precision=highest))).reshape(groups_here, CLIP_LEN, D)
    branch_one = low_back(jnp.einsum('gtd,de->gte', attended, out_weight, precision=highest))
    residual = tokens + layer_scale_one * branch_one
    normed_two = low(layer_norm(residual, norm_gain_two))
    gate_up = low_back(jnp.einsum('gtd,df->gtf', normed_two, gate_up_weight, precision=highest))
    activated = low(jax.nn.silu(gate_up[..., :FF]) * gate_up[..., FF:])
    branch_two = low_back(jnp.einsum('gtf,df->gtd', activated, down_weight_t, precision=highest))
    return residual + layer_scale_two * branch_two

def reference(frames, out_grad, qkv_weight, out_weight, gate_up_weight, down_weight_t, norm_gain_one, norm_gain_two, layer_scale_one, layer_scale_two, speaker, clip_bounds):
    weights = tuple((weight_array.astype(jnp.float32) for weight_array in (qkv_weight, out_weight, gate_up_weight, down_weight_t, norm_gain_one, norm_gain_two, layer_scale_one, layer_scale_two)))
    group_size = max((option for option in (8, 4, 2, 1) if STREAMS % option == 0))
    group_count = STREAMS // group_size
    shaped = (group_count, group_size, CLIP_LEN, D)

    def group_step(running, inputs):
        tokens, cotangent, bounds_here = inputs

        def forward(token_values, *params):
            return block_forward(token_values, *params, bounds_here)
        result, pullback = jax.vjp(forward, tokens.astype(jnp.float32), *weights)
        gradients = pullback(cotangent.astype(jnp.float32))
        updated = tuple((old_sum + new_part for old_sum, new_part in zip(running, gradients[1:])))
        return (updated, (result, gradients[0]))
    initial = tuple((jnp.zeros(weight_array.shape, jnp.float32) for weight_array in weights))
    sums_out, (results, input_grads) = lax.scan(group_step, initial, (frames.reshape(shaped), out_grad.reshape(shaped), clip_bounds.reshape(group_count, group_size, 2)))
    results = results.reshape(STREAMS, CLIP_LEN, D)
    frame_power = lax.optimization_barrier(jnp.sum(results * results, axis=1))
    one_hot = (speaker[:, None] == jnp.arange(SPEAKERS, dtype=jnp.int32)[None, :]).astype(jnp.float32)
    power_sums = jnp.dot(one_hot.T, frame_power, precision=highest)
    frame_counts = lax.optimization_barrier(jnp.sum(one_hot, axis=0)) * CLIP_LEN
    speaker_power = power_sums / jnp.maximum(frame_counts, 1.0)[:, None]
    return (results.astype(jnp.bfloat16), speaker_power, input_grads.reshape(STREAMS, CLIP_LEN, D).astype(jnp.bfloat16), sums_out[0], sums_out[1], sums_out[2], sums_out[3], sums_out[4], sums_out[5], sums_out[6], sums_out[7])
```

```python
import math

import jax
import jax.numpy as jnp
from jax import lax
from jax.sharding import Mesh, PartitionSpec as P

HEADS = 16
WINDOW = 128
CLIP_LEN = 512
SPEAKERS = 128

bf16 = jnp.bfloat16
f32 = jnp.float32
highest = lax.Precision.HIGHEST

FAR, NEAR, PAIR, CORE = "far", "near", "pair", "core"
ALL = (FAR, NEAR, PAIR, CORE)
SWAP = [(0, 1), (1, 0)]


def swap(x, axis):
    return lax.ppermute(x, axis, SWAP)


def dot(a, b):
    return jnp.dot(a, b, preferred_element_type=f32)


def dot_t(a, b):
    return lax.dot_general(a, b, (((1,), (1,)), ((), ())), preferred_element_type=f32)


def tdot(a, b):
    return lax.dot_general(a, b, (((0,), (0,)), ((), ())), preferred_element_type=f32)


def gather_tokens(x):
    across = swap(x, PAIR)
    both = jnp.concatenate([x, across], axis=0)
    other = swap(both, CORE)
    k = x.shape[0]
    return jnp.concatenate([x, other[:k], across, other[k:]], axis=0)


def reorder(x, order):
    blocks = jnp.split(x, 4, axis=0)
    return jnp.concatenate([blocks[i] for i in order], axis=0)


def scatter_tokens(x):
    blocks = jnp.split(x, 4, axis=0)
    got = swap(jnp.concatenate([blocks[1], blocks[3]], axis=0).astype(bf16), CORE).astype(f32)
    k = blocks[0].shape[0]
    keep = blocks[0] + got[:k]
    send = blocks[2] + got[k:]
    return keep + swap(send.astype(bf16), PAIR).astype(f32)


def own_first(x, near, axis):
    shape = x.shape
    width = shape[axis] // (2 * lax.axis_size(FAR))
    lead = shape[:axis]
    tail = shape[axis + 1 :]
    parts = x.reshape(lead + (shape[axis] // (2 * width), 2, width) + tail)
    first = lax.index_in_dim(parts, 0, axis + 1, keepdims=False)
    second = lax.index_in_dim(parts, 1, axis + 1, keepdims=False)
    half = lead + (shape[axis] // 2,) + tail
    first = first.reshape(half)
    second = second.reshape(half)
    return jnp.concatenate(
        [jnp.where(near == 0, first, second), jnp.where(near == 0, second, first)], axis=axis
    )


def natural(x, near, axis):
    own, other = jnp.split(x, 2, axis=axis)
    return merge(own, other, near, axis, x.shape[axis] // (2 * lax.axis_size(FAR)))


def slice_natural(own, other, near, axis):
    return merge(own, other, near, axis, own.shape[axis] * 4 // lax.axis_size(FAR))


def merge(own, other, near, axis, width):
    shape = own.shape[:axis] + (2 * own.shape[axis],) + own.shape[axis + 1 :]
    lead = shape[:axis]
    tail = shape[axis + 1 :]
    first = jnp.where(near == 0, own, other)
    second = jnp.where(near == 0, other, own)
    grid = lead + (shape[axis] // (2 * width), width) + tail
    return jnp.stack([first.reshape(grid), second.reshape(grid)], axis=axis + 1).reshape(shape)


def rotate(vector, cosine, sine_table):
    half_size = vector.shape[-1] // 2
    lower = vector[..., :half_size]
    upper = vector[..., half_size:]
    return jnp.concatenate(
        [lower * cosine - upper * sine_table, upper * cosine + lower * sine_table], axis=-1
    )


def norm_stats(values):
    centred = values - jnp.mean(values, axis=1, keepdims=True)
    inverse = lax.rsqrt(jnp.mean(centred * centred, axis=1, keepdims=True) + 1e-05)
    return centred * inverse, inverse


def norm_backward(incoming, unit_rows, inverse, norm_gain):
    scaled = incoming * norm_gain
    gain_grad = jnp.sum(incoming * unit_rows, axis=0)
    outgoing = inverse * (
        scaled
        - jnp.mean(scaled, axis=1, keepdims=True)
        - unit_rows * jnp.mean(scaled * unit_rows, axis=1, keepdims=True)
    )
    return outgoing, gain_grad


def gather_rows(block):
    count = lax.axis_size(FAR)
    mine = lax.all_to_all(
        jnp.broadcast_to(block[None], (count,) + block.shape), FAR, 0, 0, tiled=True
    ).reshape(count * block.shape[0], block.shape[1])
    return mine, swap(mine, NEAR)


def scatter_rows(left, right):
    half = left.shape[1] // 2
    other = swap(tdot(left[:, half:], right).astype(bf16), NEAR)
    total = (tdot(left[:, :half], right) + other.astype(f32)).astype(bf16)
    count = lax.axis_size(FAR)
    parts = lax.all_to_all(
        total.reshape(count, half // count, right.shape[1]), FAR, 0, 0, tiled=True
    )
    return jnp.sum(parts.astype(f32), axis=0)


def body(
    frames,
    out_grad,
    qkv_weight,
    out_weight,
    gate_up_weight,
    down_weight_t,
    norm_gain_one,
    norm_gain_two,
    layer_scale_one,
    layer_scale_two,
    speaker,
    clip_bounds,
):
    streams, shard_len, width = frames.shape
    near = lax.axis_index(NEAR)
    pair = lax.axis_index(PAIR)
    core = lax.axis_index(CORE)
    shard = pair * 2 + core
    rows = qkv_weight.shape[0]
    group = width // 4
    hidden = gate_up_weight.shape[1] // 8
    head_size = width // HEADS
    heads_here = HEADS // 4
    scale_factor = head_size ** (-0.5)
    narrow = (PAIR, CORE)

    qkv_cols = qkv_weight.reshape(rows, 3, 4, group).transpose(2, 0, 1, 3).reshape(4, rows, 3 * group)
    out_cols = out_weight.reshape(rows, 4, group).transpose(1, 0, 2)
    slice_a = lax.all_to_all(
        jnp.concatenate([qkv_cols, out_cols], axis=2), narrow, 0, 0, tiled=True
    ).reshape(4 * rows, 4 * group)
    gate_up_cols = (
        gate_up_weight.reshape(rows, 2, 4, hidden).transpose(2, 0, 1, 3).reshape(4, rows, 2 * hidden)
    )
    down_cols = down_weight_t.reshape(rows, 4, hidden).transpose(1, 0, 2)
    slice_b = lax.all_to_all(
        jnp.concatenate([gate_up_cols, down_cols], axis=2), narrow, 0, 0, tiled=True
    ).reshape(4 * rows, 3 * hidden)
    a_own, a_other = gather_rows(slice_a)
    b_own, b_other = gather_rows(slice_b)
    weights_a = jnp.concatenate([a_own, a_other], axis=0)
    weights_b = jnp.concatenate([b_own, b_other], axis=0)
    qkv_here = weights_a[:, : 3 * group]
    gate_up_here = weights_b[:, : 2 * hidden]
    down_here = weights_b[:, 2 * hidden :]

    gain_one = own_first(norm_gain_one, near, 0)
    gain_two = own_first(norm_gain_two, near, 0)
    scale_one = own_first(layer_scale_one, near, 0)
    scale_two = own_first(layer_scale_two, near, 0)
    frames_here = own_first(frames.reshape(shard_len, width), near, 1)
    grad_here = own_first(out_grad.reshape(shard_len, width), near, 1)

    source = gather_tokens(frames_here).astype(f32)
    grad_rows = gather_tokens(grad_here).astype(f32)
    token_count = source.shape[0]

    unit_one, inverse_one = norm_stats(source)
    normed_one = (unit_one * gain_one).astype(bf16)
    projected = dot(normed_one, qkv_here)

    block = shard ^ jnp.arange(4, dtype=jnp.int32)
    positions = (block[:, None] * shard_len + jnp.arange(shard_len, dtype=jnp.int32)[None]).reshape(-1)
    half_size = head_size // 2
    inverse_freq = jnp.exp(
        jnp.arange(half_size, dtype=f32) * (-math.log(10000.0) / half_size)
    )
    angles = positions.astype(f32)[:, None] * inverse_freq[None, :]
    cosine = jnp.cos(angles)[:, None, :]
    sine = jnp.sin(angles)[:, None, :]
    segment = (positions >= clip_bounds[0, 0]).astype(jnp.int32) + (
        positions >= clip_bounds[0, 1]
    ).astype(jnp.int32)
    allowed = (jnp.abs(positions[:, None] - positions[None, :]) <= WINDOW) & (
        segment[:, None] == segment[None, :]
    )
    head_shape = (token_count, heads_here, head_size)
    queries = rotate(projected[:, :group].reshape(head_shape), cosine, sine).astype(bf16)
    keys = rotate(projected[:, group : 2 * group].reshape(head_shape), cosine, sine).astype(bf16)
    values = projected[:, 2 * group :].astype(bf16).reshape(head_shape)

    scores = jnp.einsum("qhe,khe->hqk", queries, keys, preferred_element_type=f32) * scale_factor
    scores = jnp.where(allowed[None], scores, -1e30)
    peak = jnp.max(scores, axis=2, keepdims=True)
    exponent = jnp.exp(scores - peak)
    probs = exponent / jnp.sum(exponent, axis=2, keepdims=True)
    probs_low = probs.astype(bf16)
    attended = (
        jnp.einsum("hqk,khe->qhe", probs_low, values, preferred_element_type=f32)
        .astype(bf16)
        .reshape(token_count, group)
    )

    from_pair = swap(reorder(attended, (2, 3, 0, 1)), PAIR)
    from_core = swap(reorder(attended, (1, 0, 3, 2)), CORE)
    from_both = swap(reorder(from_pair, (1, 0, 3, 2)), CORE)

    def by_shard(own, core_part, pair_part, both_part, axis):
        low = jnp.where(core == 0, own, core_part)
        high = jnp.where(core == 0, core_part, own)
        far_low = jnp.where(core == 0, pair_part, both_part)
        far_high = jnp.where(core == 0, both_part, pair_part)
        return jnp.concatenate(
            [
                jnp.where(pair == 0, low, far_low),
                jnp.where(pair == 0, high, far_high),
                jnp.where(pair == 0, far_low, low),
                jnp.where(pair == 0, far_high, high),
            ],
            axis=axis,
        )

    attended_all = own_first(by_shard(attended, from_core, from_pair, from_both, 1), near, 1)

    out_slice = weights_a[:, 3 * group :]
    out_pair = swap(out_slice, PAIR)
    out_core = swap(out_slice, CORE)
    out_both = swap(out_pair, CORE)
    out_full = own_first(by_shard(out_slice, out_core, out_pair, out_both, 1), near, 1)

    branch_one = dot(attended_all, out_full)
    residual = source + scale_one * branch_one
    unit_two, inverse_two = norm_stats(residual)
    normed_two = (unit_two * gain_two).astype(bf16)
    gate_up = dot(normed_two, gate_up_here)
    gate_part = gate_up[:, :hidden]
    upward = gate_up[:, hidden:]
    sigmoid_gate = jax.nn.sigmoid(gate_part)
    silu_gate = gate_part * sigmoid_gate
    activated = (silu_gate * upward).astype(bf16)
    mlp_grad = (scale_two * grad_rows).astype(bf16)
    act_grad = dot(mlp_grad, down_here)
    gate_grad = act_grad * upward * sigmoid_gate * (1.0 + gate_part * (1.0 - sigmoid_gate))
    gate_up_grad = jnp.concatenate([gate_grad, act_grad * silu_gate], axis=1).astype(bf16)
    branch_two_part = dot_t(activated, down_here)
    normed_two_part = dot_t(gate_up_grad, gate_up_here)
    sums = scatter_tokens(jnp.concatenate([branch_two_part, normed_two_part], axis=1))
    branch_two = sums[:, :width]
    normed_two_grad = sums[:, width:]

    down_grad = scatter_rows(mlp_grad, activated)
    gate_up_sum = scatter_rows(normed_two, gate_up_grad)

    grad_own = grad_rows[:shard_len]
    result = residual[:shard_len] + scale_two * branch_two
    output = natural(result.astype(bf16), near, 1).reshape(frames.shape)
    frame_power = jnp.sum(result * result, axis=0)
    scale_two_grad = jnp.sum(grad_own * branch_two, axis=0)
    back_two, gain_two_grad = norm_backward(
        normed_two_grad, unit_two[:shard_len], inverse_two[:shard_len], gain_two
    )
    residual_grad = grad_own + back_two
    scale_one_grad = jnp.sum(residual_grad * branch_one[:shard_len], axis=0)
    attn_grad = gather_tokens((scale_one * residual_grad).astype(bf16))

    far_rows = width // 8
    out_own = lax.dynamic_slice_in_dim(out_full, shard * far_rows, far_rows, 0)
    out_other = lax.dynamic_slice_in_dim(out_full, width // 2 + shard * far_rows, far_rows, 0)
    out_rows = slice_natural(out_own, out_other, near, 0)
    attended_grad = dot_t(attn_grad, out_rows).astype(bf16).reshape(head_shape)
    grad_cols_own = lax.dynamic_slice_in_dim(attn_grad, shard * far_rows, far_rows, 1)
    grad_cols_other = lax.dynamic_slice_in_dim(attn_grad, width // 2 + shard * far_rows, far_rows, 1)
    grad_cols = slice_natural(grad_cols_own, grad_cols_other, near, 1)

    prob_grad = jnp.einsum("qhe,khe->hqk", attended_grad, values, preferred_element_type=f32)
    row_delta = jnp.sum(probs * prob_grad, axis=2, keepdims=True)
    score_grad = (probs * (prob_grad - row_delta)).astype(bf16)
    query_grad = jnp.einsum("hqk,khe->qhe", score_grad, keys, preferred_element_type=f32) * scale_factor
    key_grad = jnp.einsum("hqk,qhe->khe", score_grad, queries, preferred_element_type=f32) * scale_factor
    value_grad = jnp.einsum("hqk,qhe->khe", probs_low, attended_grad, preferred_element_type=f32)
    projected_grad = jnp.concatenate(
        [
            rotate(query_grad, cosine, -sine).reshape(token_count, group),
            rotate(key_grad, cosine, -sine).reshape(token_count, group),
            value_grad.reshape(token_count, group),
        ],
        axis=1,
    ).astype(bf16)
    normed_one_grad = scatter_tokens(dot_t(projected_grad, qkv_here))
    a_sum = scatter_rows_two(normed_one, projected_grad, attended_all, grad_cols)
    back_one, gain_one_grad = norm_backward(
        normed_one_grad, unit_one[:shard_len], inverse_one[:shard_len], gain_one
    )
    frames_grad = natural((residual_grad + back_one).astype(bf16), near, 1).reshape(frames.shape)

    def everywhere(vectors):
        count = lax.axis_size(FAR) * 8
        return lax.all_to_all(
            jnp.broadcast_to(vectors[None], (count,) + vectors.shape), ALL, 0, 0, tiled=True
        )

    speaker_row = jnp.broadcast_to(speaker.astype(f32)[0], (width,))
    early = everywhere(
        jnp.stack(
            [
                natural(frame_power, near, 0),
                natural(scale_two_grad, near, 0),
                natural(gain_two_grad, near, 0),
                natural(scale_one_grad, near, 0),
                speaker_row,
            ]
        )
    )
    late = everywhere(natural(gain_one_grad, near, 0)[None])
    speakers = early[:, 4, 0].astype(jnp.int32)
    one_hot = (jnp.arange(SPEAKERS, dtype=jnp.int32)[:, None] == speakers[None, :]).astype(f32)
    power_sums = jnp.dot(one_hot, early[:, 0], precision=highest)
    frame_counts = jnp.sum(one_hot, axis=1) * shard_len
    speaker_power = power_sums / jnp.maximum(frame_counts, 1.0)[:, None]

    gate_sum, up_sum = jnp.split(gate_up_sum.astype(bf16), 2, axis=1)
    gate_up_grad_out = place_gate_up(gate_sum, up_sum, pair, core)
    qkv_sum = a_sum[:, : 3 * group]
    qkv_grad_out = place_qkv(qkv_sum.astype(bf16), pair, core)
    out_grad_out = a_sum[:, 3 * group :]
    return (
        output,
        speaker_power,
        frames_grad,
        qkv_grad_out,
        out_grad_out,
        gate_up_grad_out,
        down_grad,
        jnp.sum(late[:, 0], axis=0),
        jnp.sum(early[:, 2], axis=0),
        jnp.sum(early[:, 3], axis=0),
        jnp.sum(early[:, 1], axis=0),
    )


def scatter_rows_two(left_one, right_one, left_two, right_two):
    half = left_one.shape[1] // 2
    sent = jnp.concatenate(
        [tdot(left_one[:, half:], right_one), tdot(left_two[:, half:], right_two)], axis=1
    )
    other = swap(sent.astype(bf16), NEAR)
    kept = jnp.concatenate(
        [tdot(left_one[:, :half], right_one), tdot(left_two[:, :half], right_two)], axis=1
    )
    total = (kept + other.astype(f32)).astype(bf16)
    count = lax.axis_size(FAR)
    parts = lax.all_to_all(
        total.reshape(count, half // count, total.shape[1]), FAR, 0, 0, tiled=True
    )
    return jnp.sum(parts.astype(f32), axis=0)


def place_gate_up(gate, up, pair, core):
    narrow = (PAIR, CORE)
    shard = pair * 2 + core
    first = jnp.where(shard == 1, up, gate)
    second = jnp.where(shard == 0, up, gate)
    second = jnp.where(shard == 2, up, second)
    got_one = lax.ppermute(first, narrow, [(1, 2), (2, 1)])
    got_two = lax.ppermute(second, narrow, [(0, 2), (1, 0), (2, 3), (3, 1)])
    left = jnp.where(shard == 0, gate, jnp.where(shard == 1, got_one, got_two))
    right = jnp.where(shard == 3, up, jnp.where(shard == 2, got_one, got_two))
    return jnp.concatenate([left, right], axis=1).astype(f32)


def place_qkv(block, pair, core):
    shard = pair * 2 + core
    query, key, value = jnp.split(block, 3, axis=1)
    to_core = jnp.where(
        shard == 0, key, jnp.where(shard == 1, query, jnp.where(shard == 2, value, key))
    )
    to_pair = jnp.where(pair == 0, value, query)
    stay = jnp.where(shard == 0, query, jnp.where(shard == 3, value, key))
    got_core = swap(to_core, CORE)
    got_pair = swap(to_pair, PAIR)
    left = jnp.where(core == 0, stay, got_pair)
    right = jnp.where(core == 0, got_pair, stay)
    return jnp.concatenate([left, got_core, right], axis=1).astype(f32)


def solution(mesh):
    wide = mesh.shape["wide"]
    split = Mesh(mesh.devices.reshape(wide // 2, 2, 2, 2), ALL)
    both = (FAR, NEAR)
    narrow = (PAIR, CORE)
    placed = (
        P(both, narrow, None),
        P(both, narrow, None),
        P(ALL, None),
        P(ALL, None),
        P(ALL, None),
        P(ALL, None),
        P(),
        P(),
        P(),
        P(),
        P(both),
        P(both, None),
    )
    return jax.shard_map(
        body,
        mesh=split,
        in_specs=placed,
        out_specs=(
            P(both, narrow, None),
            P(),
            P(both, narrow, None),
            P(both, narrow),
            P(both, narrow),
            P(both, narrow),
            P(both, narrow),
            P(),
            P(),
            P(),
            P(),
        ),
        check_vma=False,
    )
```

```python
import functools
import math

import jax
import jax.numpy as jnp
from jax import lax
from jax.experimental import pallas as pl
from jax.experimental.pallas import tpu as pltpu
from jax.sharding import Mesh, PartitionSpec as P

HEADS = 16
WINDOW = 128
CLIP_LEN = 512
SPEAKERS = 128

bf16 = jnp.bfloat16
f32 = jnp.float32
highest = lax.Precision.HIGHEST

FAR, NEAR, PAIR, CORE = "far", "near", "pair", "core"
ALL = (FAR, NEAR, PAIR, CORE)
SWAP = [(0, 1), (1, 0)]


def swap(x, axis):
    return lax.ppermute(x, axis, SWAP)


def dot(a, b):
    return jnp.dot(a, b, preferred_element_type=f32)


def dot_t(a, b):
    return lax.dot_general(a, b, (((1,), (1,)), ((), ())), preferred_element_type=f32)


def tdot(a, b):
    return lax.dot_general(a, b, (((0,), (0,)), ((), ())), preferred_element_type=f32)


def far_count():
    return lax.axis_size(FAR)


def piece_index():
    far, near = lax.axis_index(FAR), lax.axis_index(NEAR)
    return [(far ^ k) * 2 + (near ^ i) for i in range(2) for k in range(far_count())]


def to_pieces(x, axis):
    size = x.shape[axis] // (2 * far_count())
    return jnp.concatenate(
        [lax.dynamic_slice_in_dim(x, i * size, size, axis) for i in piece_index()], axis=axis
    )


def from_pieces(x, axis):
    count = far_count()
    far, near = lax.axis_index(FAR), lax.axis_index(NEAR)
    size = x.shape[axis] // (2 * count)
    return jnp.concatenate(
        [
            lax.dynamic_slice_in_dim(x, ((near ^ i) * count + (far ^ k)) * size, size, axis)
            for k in range(count)
            for i in range(2)
        ],
        axis=axis,
    )


def swap_far(x, bit):
    return lax.ppermute(x, FAR, [(i, i ^ bit) for i in range(far_count())])


def gather_rows(block):
    own = [block]
    for j in range(1, far_count()):
        low = j & -j
        own.append(swap_far(own[j ^ low], low))
    return own + [swap(x, NEAR) for x in own]


def scatter_parts(parts):
    count = far_count()
    total = [
        parts[0, k] + swap(parts[1, k].astype(bf16), NEAR).astype(f32) for k in range(count)
    ]
    for j in range(count - 1, 0, -1):
        low = j & -j
        total[j ^ low] = total[j ^ low] + swap_far(total[j].astype(bf16), low).astype(f32)
    return total[0]


def shard_columns(x):
    core = lax.axis_index(CORE)
    pair = lax.axis_index(PAIR)
    slices = [[x[0], x[1]], [x[2], x[3]]]

    def pick(flag, a, b):
        return jnp.where(flag == 0, a, b)

    stay = jnp.stack([pick(core, s[0], s[1]) for s in slices])
    send = jnp.stack([pick(core, s[1], s[0]) for s in slices])
    got = swap(send, CORE)
    rows = jnp.concatenate([pick(core, stay, got), pick(core, got, stay)], axis=1)
    stay = pick(pair, rows[0], rows[1])
    got = swap(pick(pair, rows[1], rows[0]), PAIR)
    return jnp.concatenate([pick(pair, stay, got), pick(pair, got, stay)], axis=0)


BLOCK = 128
PIECES = 8


def call(kernel, name, outs, ins, scratch=(), smem=1, anywhere=(), megabytes=40):
    specs = []
    for i in range(len(ins)):
        if i < smem:
            specs.append(pl.BlockSpec(memory_space=pltpu.SMEM))
        elif i in anywhere:
            specs.append(pl.BlockSpec(memory_space=pl.ANY))
        else:
            specs.append(pl.BlockSpec(memory_space=pltpu.VMEM))
    return pl.pallas_call(
        kernel,
        out_shape=[jax.ShapeDtypeStruct(shape, dtype) for shape, dtype in outs],
        in_specs=specs,
        out_specs=[pl.BlockSpec(memory_space=pltpu.VMEM)] * len(outs),
        scratch_shapes=list(scratch),
        compiler_params=pltpu.CompilerParams(vmem_limit_bytes=megabytes * 2**20),
        cost_estimate=pl.CostEstimate(flops=1000, bytes_accessed=1000, transcendentals=0),
        name=name,
    )(*ins)


def feature_block(wide, piece):
    return wide ^ ((piece % 4) * 2 + piece // 4)


def lanes(block, size=BLOCK):
    return pl.ds(pl.multiple_of(block * size, size), size)


def normalise(x):
    centred = x - jnp.mean(x, axis=1, keepdims=True)
    inverse = lax.rsqrt(jnp.mean(centred * centred, axis=1, keepdims=True) + 1e-05)
    return centred * inverse, inverse


def token_blocks(own, across, other):
    return [own[...], other[:BLOCK, :], across[...], other[BLOCK:, :]]


def permute_lanes(wide, source, target):
    for j in range(PIECES):
        target[:, j * BLOCK : (j + 1) * BLOCK] = source[:, lanes(feature_block(wide, j))]


def turn(x, cos, sin, sign):
    lane = lax.broadcasted_iota(jnp.int32, x.shape, 1)
    lower = (lane & 63) < 32
    partner = jnp.where(lower, pltpu.roll(x, BLOCK - 32, 1), pltpu.roll(x, 32, 1))
    return x * cos + (sign * partner) * sin


def allowed_pairs(shard, block, first, second, keys):
    row = lax.broadcasted_iota(jnp.int32, (BLOCK, keys), 0)
    lane = lax.broadcasted_iota(jnp.int32, (BLOCK, keys), 1)
    query = (shard ^ block) * BLOCK + row
    key = (shard ^ (lane // BLOCK)) * BLOCK + lane % BLOCK

    def segment(position):
        return (position >= first).astype(jnp.int32) + (position >= second).astype(jnp.int32)

    return (jnp.abs(query - key) <= WINDOW) & (segment(query) == segment(key))


def half_mask(head, shape):
    lane = lax.broadcasted_iota(jnp.int32, shape, 1)
    return (lane // 64) == head


def attend_kernel(index, own, across, other, *refs):
    pieces = refs[:PIECES]
    gain, cos, sin, normed, qkv, stat, att, att_core, att_pair, weight, left = refs[PIECES:]
    wide, shard, first, second = index[0], index[1], index[2], index[3]
    for b, x in enumerate(token_blocks(own, across, other)):
        unit, _ = normalise(x.astype(f32))
        normed[b * BLOCK : (b + 1) * BLOCK, :] = (unit * gain[...]).astype(bf16)
    permute_lanes(wide, normed, left)
    for j in range(PIECES):
        weight[j * BLOCK : (j + 1) * BLOCK, :] = pieces[j][:, : weight.shape[1]]
    group = weight.shape[1] // 3
    tiles = group // BLOCK
    for part in range(3):
        x = dot(left[...], weight[:, part * group : (part + 1) * group])
        for t in range(tiles):
            y = x[:, t * BLOCK : (t + 1) * BLOCK]
            if part < 2:
                y = turn(y, cos[...], sin[...], 1.0)
            at = part * group + t * BLOCK
            qkv[:, at : at + BLOCK] = y.astype(bf16)
    keys = normed.shape[0]
    scale = 64**-0.5
    for b in range(4):
        here = slice(b * BLOCK, (b + 1) * BLOCK)
        mask = allowed_pairs(shard, b, first, second, keys)
        stats = jnp.zeros((BLOCK, BLOCK), f32)
        for t in range(tiles):
            query = qkv[here, t * BLOCK : (t + 1) * BLOCK]
            key = qkv[:, group + t * BLOCK : group + (t + 1) * BLOCK]
            value = qkv[:, 2 * group + t * BLOCK : 2 * group + (t + 1) * BLOCK]
            merged = None
            for h in range(2):
                keep = half_mask(h, query.shape)
                scores = dot_t(jnp.where(keep, query, jnp.zeros_like(query)), key) * scale
                scores = jnp.where(mask, scores, -1e30)
                peak = jnp.max(scores, axis=1, keepdims=True)
                exponent = jnp.exp(scores - peak)
                total = jnp.sum(exponent, axis=1, keepdims=True)
                probs = (exponent * (1.0 / total)).astype(bf16)
                lane = lax.broadcasted_iota(jnp.int32, stats.shape, 1)
                stats = jnp.where(lane == 2 * t + h, peak + jnp.log(total), stats)
                part = dot(probs, value)
                merged = part if merged is None else jnp.where(keep, part, merged)
            merged = merged.astype(bf16)
            cols = slice(t * BLOCK, (t + 1) * BLOCK)
            att[here, cols] = merged
            to_core, to_pair = b ^ 1, b ^ 2
            att_core[to_core * BLOCK : (to_core + 1) * BLOCK, cols] = merged
            att_pair[to_pair * BLOCK : (to_pair + 1) * BLOCK, cols] = merged
        stat[here, :] = stats


def residual_kernel(
    index, own, across, other, att0, att1, att2, att3, out0, out1, out2, out3, scale_one, gain_two,
    normed, att_pieces, residual_own, branch_own, stacked, branch,
):
    wide, shard = index[0], index[1]
    for m, part in enumerate((att0, att1, att2, att3)):
        stacked[m] = part[...]
    for j in range(PIECES):
        block = feature_block(wide, j)
        att_pieces[:, j * BLOCK : (j + 1) * BLOCK] = stacked[shard ^ (block // 2), :, lanes(block % 2)]
    group = out0.shape[1]
    for m, part in enumerate((out0, out1, out2, out3)):
        branch[:, lanes(shard ^ m, group)] = dot(att_pieces[...], part[...])
    for b, x in enumerate(token_blocks(own, across, other)):
        here = slice(b * BLOCK, (b + 1) * BLOCK)
        total = x.astype(f32) + scale_one[...] * branch[here, :]
        unit, _ = normalise(total)
        normed[here, :] = (unit * gain_two[...]).astype(bf16)
        if b == 0:
            residual_own[...] = total
            branch_own[...] = branch[here, :]


def mlp_kernel(index, normed, own, across, other, *refs):
    pieces = refs[:PIECES]
    scale_two, activated, gate_up_grad, mlp_grad, keep, send, weight, left, grad, total, sems = refs[PIECES:]
    wide = index[0]
    copies = [
        pltpu.make_async_copy(pieces[j], weight.at[pl.ds(j * BLOCK, BLOCK), :], sems.at[j])
        for j in range(PIECES)
    ]
    for copy in copies:
        copy.start()
    for b, x in enumerate(token_blocks(own, across, other)):
        mlp_grad[b * BLOCK : (b + 1) * BLOCK, :] = (scale_two[...] * x.astype(f32)).astype(bf16)
    permute_lanes(wide, normed, left)
    permute_lanes(wide, mlp_grad, grad)
    for copy in copies:
        copy.wait()
    width = normed.shape[1]
    hidden = activated.shape[1]
    chunk = 256
    for h in range(hidden // chunk):
        gate_at = slice(h * chunk, (h + 1) * chunk)
        up_at = slice(hidden + h * chunk, hidden + (h + 1) * chunk)
        down_at = slice(2 * hidden + h * chunk, 2 * hidden + (h + 1) * chunk)
        gate = dot(left[...], weight[:, gate_at])
        up = dot(left[...], weight[:, up_at])
        act_grad = dot(grad[...], weight[:, down_at])
        sigmoid = 1.0 / (1.0 + jnp.exp(-gate))
        silu = gate * sigmoid
        act = (silu * up).astype(bf16)
        activated[:, gate_at] = act
        gate_grad = (act_grad * up * sigmoid * (1.0 + gate * (1.0 - sigmoid))).astype(bf16)
        up_grad = (act_grad * silu).astype(bf16)
        gate_up_grad[:, gate_at] = gate_grad
        gate_up_grad[:, up_at] = up_grad
        branch = dot_t(act, weight[:, down_at])
        back = dot_t(gate_grad, weight[:, gate_at]) + dot_t(up_grad, weight[:, up_at])
        if h == 0:
            total[:, :width] = branch
            total[:, width:] = back
        else:
            total[:, :width] += branch
            total[:, width:] += back
    keep[:BLOCK, :] = total[:BLOCK, :]
    keep[BLOCK:, :] = total[2 * BLOCK : 3 * BLOCK, :]
    send[:BLOCK, :] = total[BLOCK : 2 * BLOCK, :].astype(bf16)
    send[BLOCK:, :] = total[3 * BLOCK :, :].astype(bf16)


def weight_grad_kernel(half, natural, count, index, *refs):
    lefts, rights, outs = refs[:count], refs[count : 2 * count], refs[2 * count : 2 * count + 4]
    wide = index[0]
    for k in range(4):
        piece = half * 4 + k
        at = 0
        for left, right, order in zip(lefts, rights, natural):
            block = feature_block(wide, piece) if order else piece
            cols = lanes(block) if order else slice(piece * BLOCK, (piece + 1) * BLOCK)
            width = right.shape[1]
            outs[k][:, at : at + width] = tdot(left[:, cols], right[...]).astype(outs[k].dtype)
            at += width


def middle_kernel(
    index, keep, got_core, got_pair, own_grad, residual, branch_one, scale_one, scale_two, gain_two,
    output, rows, residual_grad, attn_grad, sums,
):
    wide = index[0]
    width = residual.shape[1]
    for half in range(2):
        for j in range(PIECES):
            at = slice(half * width + j * BLOCK, half * width + (j + 1) * BLOCK)
            sums[half, :, lanes(feature_block(wide, j))] = (
                keep[:, at] + got_core[:, at].astype(f32) + got_pair[:, at].astype(f32)
            )
    branch_two = sums[0]
    incoming = sums[1]
    grad = own_grad[...].astype(f32)
    result = residual[...] + scale_two[...] * branch_two
    output[...] = result.astype(bf16)
    unit, inverse = normalise(residual[...])
    scaled = incoming * gain_two[...]
    back = inverse * (
        scaled
        - jnp.mean(scaled, axis=1, keepdims=True)
        - unit * jnp.mean(scaled * unit, axis=1, keepdims=True)
    )
    total = grad + back
    residual_grad[...] = total
    attn_grad[...] = (scale_one[...] * total).astype(bf16)
    rows[0:1, :] = jnp.sum(result * result, axis=0, keepdims=True)
    rows[1:2, :] = jnp.sum(grad * branch_two, axis=0, keepdims=True)
    rows[2:3, :] = jnp.sum(incoming * unit, axis=0, keepdims=True)
    rows[3:4, :] = jnp.sum(total * branch_one[...], axis=0, keepdims=True)
    rows[4:5, :] = jnp.full((1, width), index[4], jnp.int32).astype(f32)
    rows[5:8, :] = jnp.zeros((3, width), f32)


def attend_back_kernel(index, own, across, other, out0, out1, out2, out3, qkv, att, stat, cos, sin, *refs):
    pieces = refs[:PIECES]
    projected, grad_cols, keep, send, weight, grads, att_grad, probs_all, score_all = refs[PIECES:]
    wide, shard, first, second = index[0], index[1], index[2], index[3]
    for j in range(PIECES):
        weight[j * BLOCK : (j + 1) * BLOCK, :] = pieces[j][:, : weight.shape[1]]
    for b, x in enumerate(token_blocks(own, across, other)):
        grads[b * BLOCK : (b + 1) * BLOCK, :] = x
    group = out0.shape[1]
    tiles = group // BLOCK
    grad_cols[...] = grads[:, lanes(shard, group)]
    for t in range(tiles):
        relative = wide ^ (shard * 2 + t)
        piece = (relative % 2) * 4 + relative // 2
        total = None
        for m, part in enumerate((out0, out1, out2, out3)):
            product = dot_t(grads[:, lanes(shard ^ m, group)], part[lanes(piece), :])
            total = product if total is None else total + product
        att_grad[:, t * BLOCK : (t + 1) * BLOCK] = total.astype(bf16)
    keys = qkv.shape[0]
    scale = 64**-0.5
    for t in range(tiles):
        cols = slice(t * BLOCK, (t + 1) * BLOCK)
        key = qkv[:, group + t * BLOCK : group + (t + 1) * BLOCK]
        value = qkv[:, 2 * group + t * BLOCK : 2 * group + (t + 1) * BLOCK]
        query_grad = [None] * 4
        key_grad = None
        value_grad = None
        for h in range(2):
            for b in range(4):
                here = slice(b * BLOCK, (b + 1) * BLOCK)
                mask = allowed_pairs(shard, b, first, second, keys)
                query = qkv[here, cols]
                grad = att_grad[here, cols]
                keep_lanes = half_mask(h, query.shape)
                none = jnp.zeros_like(query)
                scores = dot_t(jnp.where(keep_lanes, query, none), key) * scale
                probs = jnp.where(mask, jnp.exp(scores - stat[here, 2 * t + h : 2 * t + h + 1]), 0.0)
                grad_here = jnp.where(keep_lanes, grad, none)
                prob_grad = dot_t(grad_here, value)
                delta = jnp.sum(probs * prob_grad, axis=1, keepdims=True)
                score_grad = (probs * (prob_grad - delta)).astype(bf16)
                probs_all[here, :] = probs.astype(bf16)
                score_all[here, :] = score_grad
                part = dot(score_grad, key)
                query_grad[b] = part if h == 0 else jnp.where(keep_lanes, part, query_grad[b])
            k_part = tdot(score_all[...], qkv[:, cols])
            v_part = tdot(probs_all[...], att_grad[:, cols])
            keep_all = half_mask(h, k_part.shape)
            key_grad = k_part if h == 0 else jnp.where(keep_all, k_part, key_grad)
            value_grad = v_part if h == 0 else jnp.where(keep_all, v_part, value_grad)
        for b in range(4):
            here = slice(b * BLOCK, (b + 1) * BLOCK)
            projected[here, cols] = turn(
                query_grad[b] * scale, cos[here, :], sin[here, :], -1.0
            ).astype(bf16)
        projected[:, group + t * BLOCK : group + (t + 1) * BLOCK] = turn(
            key_grad * scale, cos[...], sin[...], -1.0
        ).astype(bf16)
        projected[:, 2 * group + t * BLOCK : 2 * group + (t + 1) * BLOCK] = value_grad.astype(bf16)
    for b, target in enumerate((keep, send, keep, send)):
        at = (b // 2) * BLOCK
        target[at : at + BLOCK, :] = dot_t(
            projected[b * BLOCK : (b + 1) * BLOCK, :], weight[...]
        ).astype(target.dtype)


def last_kernel(
    index, keep, got_core, got_pair, frames, residual_grad, gain_one, frames_grad, rows, sums
):
    wide = index[0]
    width = residual_grad.shape[1]
    for j in range(PIECES):
        at = slice(j * BLOCK, (j + 1) * BLOCK)
        sums[:, lanes(feature_block(wide, j))] = (
            keep[:, at] + got_core[:, at].astype(f32) + got_pair[:, at].astype(f32)
        )
    incoming = sums[...]
    unit, inverse = normalise(frames[...].astype(f32))
    scaled = incoming * gain_one[...]
    back = inverse * (
        scaled
        - jnp.mean(scaled, axis=1, keepdims=True)
        - unit * jnp.mean(scaled * unit, axis=1, keepdims=True)
    )
    frames_grad[...] = (residual_grad[...] + back).astype(bf16)
    rows[0:1, :] = jnp.sum(incoming * unit, axis=0, keepdims=True)
    rows[1:8, :] = jnp.zeros((7, width), f32)


def kernel_pieces(pieces):
    if len(pieces) == PIECES:
        return pieces, lax.axis_index(FAR) * 2 + lax.axis_index(NEAR)
    ordered = from_pieces(jnp.concatenate(pieces, axis=0), 0)
    size = ordered.shape[0] // PIECES
    split = [ordered[b * size : (b + 1) * size] for b in range(PIECES)]
    return [split[(j % 4) * 2 + j // 4] for j in range(PIECES)], jnp.int32(0)


def sum_rows(own, other):
    count = far_count()
    if count == 4:
        parts = {(i, k): (own, other)[i][k] for i in range(2) for k in range(4)}
        return scatter_parts(parts)
    ordered = [(own + other)[(b % 2) * 4 + b // 2] for b in range(PIECES)]
    pieces = to_pieces(jnp.concatenate([x.astype(f32) for x in ordered], axis=0), 0)
    size = pieces.shape[0] // (2 * count)
    parts = {}
    for i in range(2):
        for k in range(count):
            at = (i * count + k) * size
            parts[i, k] = pieces[at : at + size]
    return scatter_parts(parts)


def weight_grads(index, lefts, rights, natural):
    columns = sum(right.shape[1] for right in rights)

    def half(which, dtype):
        return call(
            functools.partial(weight_grad_kernel, which, natural, len(lefts)),
            "weight_grad",
            [((BLOCK, columns), dtype)] * 4,
            [index, *lefts, *rights],
        )

    other = half(1, bf16)
    return sum_rows(half(0, f32), other)


def body(
    frames,
    out_grad,
    qkv_weight,
    out_weight,
    gate_up_weight,
    down_weight_t,
    norm_gain_one,
    norm_gain_two,
    layer_scale_one,
    layer_scale_two,
    speaker,
    clip_bounds,
):
    streams, shard_len, width = frames.shape
    pair = lax.axis_index(PAIR)
    core = lax.axis_index(CORE)
    shard = pair * 2 + core
    rows = qkv_weight.shape[0]
    group = width // 4
    hidden = gate_up_weight.shape[1] // 8
    head_size = width // HEADS
    tokens = 4 * shard_len

    qkv_cols = qkv_weight.reshape(rows, 3, 4, group).transpose(2, 0, 1, 3).reshape(4, rows, 3 * group)
    out_cols = out_weight.reshape(rows, 4, group).transpose(1, 0, 2)
    slice_a = shard_columns(jnp.concatenate([qkv_cols, out_cols], axis=2))
    gate_up_cols = gate_up_weight.reshape(rows, 2, 4, hidden).transpose(2, 0, 1, 3)
    down_cols = down_weight_t.reshape(rows, 4, hidden).transpose(1, 0, 2)
    slice_b = shard_columns(
        jnp.concatenate([gate_up_cols.reshape(4, rows, 2 * hidden), down_cols], axis=2)
    )
    pieces_a, wide = kernel_pieces(gather_rows(slice_a))
    pieces_b, _ = kernel_pieces(gather_rows(slice_b))

    index = jnp.stack([wide, shard, clip_bounds[0, 0], clip_bounds[0, 1], speaker[0]]).astype(jnp.int32)
    gain_one = norm_gain_one[None]
    gain_two = norm_gain_two[None]
    scale_one = layer_scale_one[None]
    scale_two = layer_scale_two[None]
    frames_here = frames.reshape(shard_len, width)
    grad_here = out_grad.reshape(shard_len, width)

    def spread(x):
        across = swap(x, PAIR)
        return x, across, swap(jnp.concatenate([x, across], axis=0), CORE)

    frames_all = spread(frames_here)
    grad_all = spread(grad_here)

    block = shard ^ jnp.arange(4, dtype=jnp.int32)
    positions = (block[:, None] * shard_len + jnp.arange(shard_len, dtype=jnp.int32)[None]).reshape(-1)
    half_size = head_size // 2
    lane = jnp.arange(BLOCK, dtype=jnp.int32)
    inverse_freq = jnp.exp((lane % half_size).astype(f32) * (-math.log(10000.0) / half_size))
    angles = positions.astype(f32)[:, None] * inverse_freq[None, :]
    cosine = jnp.cos(angles)
    sine = jnp.where(lane % head_size < half_size, -1.0, 1.0)[None, :] * jnp.sin(angles)

    normed_one, qkv, stat, att, att_to_core, att_to_pair = call(
        attend_kernel,
        "attend",
        [
            ((tokens, width), bf16),
            ((tokens, 3 * group), bf16),
            ((tokens, BLOCK), f32),
            ((tokens, group), bf16),
            ((tokens, group), bf16),
            ((tokens, group), bf16),
        ],
        [index, *frames_all, *pieces_a, gain_one, cosine, sine],
        [pltpu.VMEM((width, 3 * group), bf16), pltpu.VMEM((tokens, width), bf16)],
    )
    att_pair = swap(att_to_pair, PAIR)
    att_core = swap(att_to_core, CORE)
    blocks = jnp.split(att_pair, 4, axis=0)
    att_both = swap(jnp.concatenate([blocks[i] for i in (1, 0, 3, 2)], axis=0), CORE)

    out_own = jnp.concatenate([x[:, 3 * group :] for x in pieces_a], axis=0)
    out_pair = swap(out_own, PAIR)
    outs = (out_own, swap(out_own, CORE), out_pair, swap(out_pair, CORE))

    normed_two, att_pieces, residual, branch_one = call(
        residual_kernel,
        "residual",
        [
            ((tokens, width), bf16),
            ((tokens, width), bf16),
            ((shard_len, width), f32),
            ((shard_len, width), f32),
        ],
        [index, *frames_all, att, att_core, att_pair, att_both, *outs, scale_one, gain_two],
        [pltpu.VMEM((4, tokens, group), bf16), pltpu.VMEM((tokens, width), f32)],
    )

    activated, gate_up_grad, mlp_grad, keep, send = call(
        mlp_kernel,
        "mlp",
        [
            ((tokens, hidden), bf16),
            ((tokens, 2 * hidden), bf16),
            ((tokens, width), bf16),
            ((2 * shard_len, 2 * width), f32),
            ((2 * shard_len, 2 * width), bf16),
        ],
        [index, normed_two, *grad_all, *pieces_b, scale_two],
        [
            pltpu.VMEM((width, 3 * hidden), bf16),
            pltpu.VMEM((tokens, width), bf16),
            pltpu.VMEM((tokens, width), bf16),
            pltpu.VMEM((tokens, 2 * width), f32),
            pltpu.SemaphoreType.DMA((PIECES,)),
        ],
        anywhere=range(5, 5 + PIECES),
        megabytes=48,
    )

    def meet(keep, send):
        got = swap(send, CORE)
        onward = (keep[shard_len:] + got[shard_len:].astype(f32)).astype(bf16)
        return keep[:shard_len], got[:shard_len], swap(onward, PAIR)

    met = meet(keep, send)
    mlp_sum = weight_grads(index, [normed_two, mlp_grad], [gate_up_grad, activated], (True, True))
    gate_sum = mlp_sum[:, :hidden]
    up_sum = mlp_sum[:, hidden : 2 * hidden]
    down_grad = mlp_sum[:, 2 * hidden :]

    output, early_rows, residual_grad, attn_grad = call(
        middle_kernel,
        "middle",
        [
            ((shard_len, width), bf16),
            ((8, width), f32),
            ((shard_len, width), f32),
            ((shard_len, width), bf16),
        ],
        [index, *met, grad_here, residual, branch_one, scale_one, scale_two, gain_two],
        [pltpu.VMEM((2, shard_len, width), f32)],
    )
    projected_grad, grad_cols, keep, send = call(
        attend_back_kernel,
        "attend_back",
        [
            ((tokens, 3 * group), bf16),
            ((tokens, group), bf16),
            ((2 * shard_len, width), f32),
            ((2 * shard_len, width), bf16),
        ],
        [index, *spread(attn_grad), *outs, qkv, att, stat, cosine, sine, *pieces_a],
        [
            pltpu.VMEM((width, 3 * group), bf16),
            pltpu.VMEM((tokens, width), bf16),
            pltpu.VMEM((tokens, group), bf16),
            pltpu.VMEM((tokens, tokens), bf16),
            pltpu.VMEM((tokens, tokens), bf16),
        ],
    )
    met = meet(keep, send)
    a_sum = weight_grads(index, [normed_one, att_pieces], [projected_grad, grad_cols], (True, False))
    frames_grad, late_rows = call(
        last_kernel,
        "last",
        [((shard_len, width), bf16), ((8, width), f32)],
        [index, *met, frames_here, residual_grad, gain_one],
        [pltpu.VMEM((shard_len, width), f32)],
    )

    def everywhere(vectors):
        count = far_count() * 8
        return lax.all_to_all(
            jnp.broadcast_to(vectors[None], (count,) + vectors.shape), ALL, 0, 0, tiled=True
        )

    early = everywhere(early_rows[:5])
    late = everywhere(late_rows[:1])
    speakers = early[:, 4, 0].astype(jnp.int32)
    one_hot = (jnp.arange(SPEAKERS, dtype=jnp.int32)[:, None] == speakers[None, :]).astype(f32)
    power_sums = jnp.dot(one_hot, early[:, 0], precision=highest)
    frame_counts = jnp.sum(one_hot, axis=1) * shard_len
    speaker_power = power_sums / jnp.maximum(frame_counts, 1.0)[:, None]

    gate_up_grad_out = place_gate_up(gate_sum.astype(bf16), up_sum.astype(bf16), pair, core)
    qkv_grad_out = place_qkv(a_sum[:, : 3 * group].astype(bf16), pair, core)
    return (
        output.reshape(frames.shape),
        speaker_power,
        frames_grad.reshape(frames.shape),
        qkv_grad_out,
        a_sum[:, 3 * group :],
        gate_up_grad_out,
        down_grad,
        jnp.sum(late[:, 0], axis=0),
        jnp.sum(early[:, 2], axis=0),
        jnp.sum(early[:, 3], axis=0),
        jnp.sum(early[:, 1], axis=0),
    )


def place_gate_up(gate, up, pair, core):
    narrow = (PAIR, CORE)
    shard = pair * 2 + core
    first = jnp.where(shard == 1, up, gate)
    second = jnp.where(shard == 0, up, gate)
    second = jnp.where(shard == 2, up, second)
    got_one = lax.ppermute(first, narrow, [(1, 2), (2, 1)])
    got_two = lax.ppermute(second, narrow, [(0, 2), (1, 0), (2, 3), (3, 1)])
    left = jnp.where(shard == 0, gate, jnp.where(shard == 1, got_one, got_two))
    right = jnp.where(shard == 3, up, jnp.where(shard == 2, got_one, got_two))
    return jnp.concatenate([left, right], axis=1).astype(f32)


def place_qkv(block, pair, core):
    shard = pair * 2 + core
    query, key, value = jnp.split(block, 3, axis=1)
    to_core = jnp.where(
        shard == 0, key, jnp.where(shard == 1, query, jnp.where(shard == 2, value, key))
    )
    to_pair = jnp.where(pair == 0, value, query)
    stay = jnp.where(shard == 0, query, jnp.where(shard == 3, value, key))
    got_core = swap(to_core, CORE)
    got_pair = swap(to_pair, PAIR)
    left = jnp.where(core == 0, stay, got_pair)
    right = jnp.where(core == 0, got_pair, stay)
    return jnp.concatenate([left, got_core, right], axis=1).astype(f32)


def solution(mesh):
    wide = mesh.shape["wide"]
    split = Mesh(mesh.devices.reshape(wide // 2, 2, 2, 2), ALL)
    both = (FAR, NEAR)
    narrow = (PAIR, CORE)
    placed = (
        P(both, narrow, None),
        P(both, narrow, None),
        P(ALL, None),
        P(ALL, None),
        P(ALL, None),
        P(ALL, None),
        P(),
        P(),
        P(),
        P(),
        P(both),
        P(both, None),
    )
    return jax.shard_map(
        body,
        mesh=split,
        in_specs=placed,
        out_specs=(
            P(both, narrow, None),
            P(),
            P(both, narrow, None),
            P(both, narrow),
            P(both, narrow),
            P(both, narrow),
            P(both, narrow),
            P(),
            P(),
            P(),
            P(),
        ),
        check_vma=False,
    )
```

```python
import functools
import math

import jax
import jax.numpy as jnp
from jax import lax
from jax.experimental import pallas as pl
from jax.experimental.pallas import tpu as pltpu
from jax.sharding import Mesh, PartitionSpec as P

HEADS = 16
WINDOW = 128
CLIP_LEN = 512
SPEAKERS = 128

bf16 = jnp.bfloat16
f32 = jnp.float32
highest = lax.Precision.HIGHEST

FAR, NEAR, PAIR, CORE = "far", "near", "pair", "core"
ALL = (FAR, NEAR, PAIR, CORE)
SWAP = [(0, 1), (1, 0)]


def swap(x, axis):
    return lax.ppermute(x, axis, SWAP)


def dot(a, b):
    return jnp.dot(a, b, preferred_element_type=f32)


def dot_t(a, b):
    return lax.dot_general(a, b, (((1,), (1,)), ((), ())), preferred_element_type=f32)


def tdot(a, b):
    return lax.dot_general(a, b, (((0,), (0,)), ((), ())), preferred_element_type=f32)


def far_count():
    return lax.axis_size(FAR)


def piece_index():
    far, near = lax.axis_index(FAR), lax.axis_index(NEAR)
    return [(far ^ k) * 2 + (near ^ i) for i in range(2) for k in range(far_count())]


def to_pieces(x, axis):
    size = x.shape[axis] // (2 * far_count())
    return jnp.concatenate(
        [lax.dynamic_slice_in_dim(x, i * size, size, axis) for i in piece_index()], axis=axis
    )


def from_pieces(x, axis):
    count = far_count()
    far, near = lax.axis_index(FAR), lax.axis_index(NEAR)
    size = x.shape[axis] // (2 * count)
    return jnp.concatenate(
        [
            lax.dynamic_slice_in_dim(x, ((near ^ i) * count + (far ^ k)) * size, size, axis)
            for k in range(count)
            for i in range(2)
        ],
        axis=axis,
    )


def swap_far(x, bit):
    return lax.ppermute(x, FAR, [(i, i ^ bit) for i in range(far_count())])


def gather_line(block):
    own = [block]
    for j in range(1, far_count()):
        low = j & -j
        own.append(swap_far(own[j ^ low], low))
    return own


def gather_rows(block):
    own = gather_line(block)
    return own + [swap(x, NEAR) for x in own]


def scatter_parts(parts):
    count = far_count()
    total = [
        parts[0, k] + swap(parts[1, k].astype(bf16), NEAR).astype(f32) for k in range(count)
    ]
    for j in range(count - 1, 0, -1):
        low = j & -j
        total[j ^ low] = total[j ^ low] + swap_far(total[j].astype(bf16), low).astype(f32)
    return total[0]


def core_columns(x):
    core = lax.axis_index(CORE)
    slices = [[x[0], x[1]], [x[2], x[3]]]
    stay = jnp.stack([jnp.where(core == 0, s[0], s[1]) for s in slices])
    send = jnp.stack([jnp.where(core == 0, s[1], s[0]) for s in slices])
    got = swap(send, CORE)
    return jnp.concatenate([jnp.where(core == 0, stay, got), jnp.where(core == 0, got, stay)], axis=1)


def pair_columns(x):
    pair = lax.axis_index(PAIR)
    stay = jnp.where(pair == 0, x[0], x[1])
    got = swap(jnp.where(pair == 0, x[1], x[0]), PAIR)
    return jnp.concatenate([jnp.where(pair == 0, stay, got), jnp.where(pair == 0, got, stay)], axis=0)


BLOCK = 128
PIECES = 8
LINE = 4
MICROSECONDS = dict(
    attend=9, residual=3, mlp=11, middle=2, finish=2, attend_back=11, last=2, rows=1, onward=1, merge=1, weight_grad=2,
    fence=1, tick=0, totals=1, out=0,
)
RATE = 10**8


def call(kernel, name, outs, ins, scratch=(), smem=0, anywhere=(), far_outs=(), megabytes=24, after=()):
    specs = []
    given = len(ins)
    if len(after) > 0:
        inner = kernel

        def kernel(*refs):
            inner(*refs[:given], *refs[given + len(after) :])

    for i in range(len(ins)):
        if i < smem:
            specs.append(pl.BlockSpec(memory_space=pltpu.SMEM))
        elif i in anywhere:
            specs.append(pl.BlockSpec(memory_space=pltpu.HBM))
        else:
            specs.append(pl.BlockSpec(memory_space=pltpu.VMEM))
    specs += [pl.BlockSpec(memory_space=pl.ANY)] * len(after)
    return pl.pallas_call(
        kernel,
        out_shape=[jax.ShapeDtypeStruct(shape, dtype) for shape, dtype in outs],
        in_specs=specs,
        out_specs=[
            pl.BlockSpec(memory_space=pltpu.HBM if i in far_outs else pltpu.VMEM) for i in range(len(outs))
        ],
        scratch_shapes=list(scratch),
        compiler_params=pltpu.CompilerParams(vmem_limit_bytes=megabytes * 2**20),
        cost_estimate=pl.CostEstimate(
            flops=int(MICROSECONDS[name] * RATE), bytes_accessed=0, transcendentals=0
        ),
        name=name,
    )(*ins, *after)


def wide_here():
    if lax.axis_size(FAR) != LINE:
        return 0
    return lax.axis_index(FAR) * 2 + lax.axis_index(NEAR)


def far_here():
    return lax.axis_index(FAR) if lax.axis_size(FAR) == LINE else 0


def shard_here():
    return lax.axis_index(PAIR) * 2 + lax.axis_index(CORE)


def feature_block(wide, piece):
    return wide ^ ((piece % 4) * 2 + piece // 4)


def lanes(block, size=BLOCK):
    return pl.ds(pl.multiple_of(block * size, size), size)


def normalise(x):
    centred = x - jnp.mean(x, axis=1, keepdims=True)
    inverse = lax.rsqrt(jnp.mean(centred * centred, axis=1, keepdims=True) + 1e-05)
    return centred * inverse, inverse


def turn(x, cos, sin, sign):
    lane = lax.broadcasted_iota(jnp.int32, x.shape, 1)
    lower = (lane & 63) < 32
    partner = jnp.where(lower, pltpu.roll(x, BLOCK - 32, 1), pltpu.roll(x, 32, 1))
    return x * cos + (sign * partner) * sin


def allowed_pairs(shard, block, first, second, keys):
    row = lax.broadcasted_iota(jnp.int32, (BLOCK, keys), 0)
    lane = lax.broadcasted_iota(jnp.int32, (BLOCK, keys), 1)
    query = (shard ^ block) * BLOCK + row
    key = (shard ^ (lane // BLOCK)) * BLOCK + lane % BLOCK

    def segment(position):
        return (position >= first).astype(jnp.int32) + (position >= second).astype(jnp.int32)

    return (jnp.abs(query - key) <= WINDOW) & (segment(query) == segment(key))


def half_mask(head, shape):
    lane = lax.broadcasted_iota(jnp.int32, shape, 1)
    return (lane // 64) == head


def out_kernel(*refs):
    pieces, (out, sems) = refs[:PIECES], refs[PIECES:]
    group = out.shape[1]
    copies = [
        pltpu.make_async_copy(
            pieces[j].at[:, pl.ds(3 * group, group)],
            out.at[lanes(feature_block(wide_here(), j)), :],
            sems.at[j],
        )
        for j in range(PIECES)
    ]
    for copy in copies:
        copy.start()
    for copy in copies:
        copy.wait()


def attend_kernel(bounds, own, core, across, both, *refs):
    pieces = refs[:PIECES]
    gain, cos, sin, normed, qkv, stat, att, att_core, att_pair, weight, sems = refs[PIECES:]
    wide, shard, first, second = wide_here(), shard_here(), bounds[0, 0], bounds[0, 1]
    group = att.shape[1]
    copies = [
        pltpu.make_async_copy(
            pieces[j].at[:, pl.ds(0, 3 * group)], weight.at[lanes(feature_block(wide, j)), :], sems.at[j]
        )
        for j in range(PIECES)
    ]
    for copy in copies:
        copy.start()
    for b, x in enumerate((own, core, across, both)):
        unit, _ = normalise(x[...].astype(f32))
        normed[b * BLOCK : (b + 1) * BLOCK, :] = (unit * gain[...]).astype(bf16)
    for copy in copies:
        copy.wait()
    tiles = group // BLOCK
    for part in range(3):
        x = dot(normed[...], weight[:, part * group : (part + 1) * group])
        for t in range(tiles):
            y = x[:, t * BLOCK : (t + 1) * BLOCK]
            if part < 2:
                y = turn(y, cos[...], sin[...], 1.0)
            at = part * group + t * BLOCK
            qkv[:, at : at + BLOCK] = y.astype(bf16)
    keys = normed.shape[0]
    scale = 64**-0.5
    for b in range(4):
        here = slice(b * BLOCK, (b + 1) * BLOCK)
        mask = allowed_pairs(shard, b, first, second, keys)
        stats = jnp.zeros((BLOCK, BLOCK), f32)
        for t in range(tiles):
            query = qkv[here, t * BLOCK : (t + 1) * BLOCK]
            key = qkv[:, group + t * BLOCK : group + (t + 1) * BLOCK]
            value = qkv[:, 2 * group + t * BLOCK : 2 * group + (t + 1) * BLOCK]
            merged = None
            for h in range(2):
                keep = half_mask(h, query.shape)
                scores = dot_t(jnp.where(keep, query, jnp.zeros_like(query)), key) * scale
                scores = jnp.where(mask, scores, -1e30)
                peak = jnp.max(scores, axis=1, keepdims=True)
                exponent = jnp.exp(scores - peak)
                total = jnp.sum(exponent, axis=1, keepdims=True)
                probs = (exponent * (1.0 / total)).astype(bf16)
                lane = lax.broadcasted_iota(jnp.int32, stats.shape, 1)
                stats = jnp.where(lane == 2 * t + h, peak + jnp.log(total), stats)
                part = dot(probs, value)
                merged = part if merged is None else jnp.where(keep, part, merged)
            merged = merged.astype(bf16)
            cols = slice(t * BLOCK, (t + 1) * BLOCK)
            att[here, cols] = merged
            to_core, to_pair = b ^ 1, b ^ 2
            att_core[to_core * BLOCK : (to_core + 1) * BLOCK, cols] = merged
            att_pair[to_pair * BLOCK : (to_pair + 1) * BLOCK, cols] = merged
        stat[here, :] = stats


def residual_kernel(
    own, core, across, both, att0, att1, att2, att3, out0, out1, out2, out3, scale_one, gain_two,
    normed, normed_even, attended, residual_own, branch_own, branch,
):
    shard = shard_here()
    group = out0.shape[1]
    for m, part in enumerate((att0, att1)):
        attended[:, lanes(shard ^ m, group)] = part[...]
    attended[:, lanes(shard ^ 2, group)] = att2[...]
    for b in range(4):
        attended[b * BLOCK : (b + 1) * BLOCK, lanes(shard ^ 3, group)] = att3[
            (b ^ 1) * BLOCK : ((b ^ 1) + 1) * BLOCK, :
        ]
    for m, part in enumerate((out0, out1, out2, out3)):
        branch[:, lanes(shard ^ m, group)] = dot(attended[...], part[...])
    for b, x in enumerate((own, core, across, both)):
        here = slice(b * BLOCK, (b + 1) * BLOCK)
        total = x[...].astype(f32) + scale_one[...] * branch[here, :]
        unit, _ = normalise(total)
        low = (unit * gain_two[...]).astype(bf16)
        normed[here, :] = low
        if b % 2 == 0:
            normed_even[b // 2 * BLOCK : (b // 2 + 1) * BLOCK, :] = low
        if b == 0:
            residual_own[...] = total
            branch_own[...] = branch[here, :]


def mlp_kernel(normed_here, near_even, near_odd, *refs):
    grads, refs = refs[:8], refs[8:]
    pieces, scale_two, refs = refs[:LINE], refs[LINE], refs[LINE + 1 :]
    (keep, send, keep_late, send_late), outs, refs = refs[:4], refs[4 : 4 + LINE], refs[4 + LINE :]
    normed, mlp_grad, activated, gate_up_grad, weight, sems = refs
    far = far_here()
    rows = pieces[0].shape[0]
    copies = [
        pltpu.make_async_copy(pieces[k], weight.at[lanes(far ^ k, rows), :], sems.at[k]) for k in range(LINE)
    ]
    for copy in copies:
        copy.start()
    tokens = 4 * BLOCK
    normed[:tokens, :] = normed_here[...]
    for b in range(4):
        source = near_odd if b % 2 else near_even
        normed[tokens + b * BLOCK : tokens + (b + 1) * BLOCK, :] = source[b // 2 * BLOCK : (b // 2 + 1) * BLOCK, :]
    for b, x in enumerate(grads):
        mlp_grad[b * BLOCK : (b + 1) * BLOCK, :] = (scale_two[...] * x[...].astype(f32)).astype(bf16)
    for copy in copies:
        copy.wait()
    hidden = activated.shape[1]
    gate_at, up_at, down_at = [slice(i * hidden, (i + 1) * hidden) for i in range(3)]
    for stream in range(2):
        here = slice(stream * tokens, (stream + 1) * tokens)
        gate = dot(normed[here, :], weight[:, gate_at])
        up = dot(normed[here, :], weight[:, up_at])
        act_grad = dot(mlp_grad[here, :], weight[:, down_at])
        sigmoid = 1.0 / (1.0 + jnp.exp(-gate))
        silu = gate * sigmoid
        activated[here, :] = (silu * up).astype(bf16)
        gate_up_grad[here, gate_at] = (act_grad * up * sigmoid * (1.0 + gate * (1.0 - sigmoid))).astype(bf16)
        gate_up_grad[here, up_at] = (act_grad * silu).astype(bf16)
        back = dot_t(gate_up_grad[here, gate_at], weight[:, gate_at])
        back = (back + dot_t(gate_up_grad[here, up_at], weight[:, up_at])).astype(bf16)
        branch = dot_t(activated[here, :], weight[:, down_at]).astype(bf16)
        for b in range(4):
            here = slice(b * BLOCK, (b + 1) * BLOCK)
            at = stream * 2 * BLOCK + b // 2 * BLOCK
            early, late = (send, send_late) if b % 2 else (keep, keep_late)
            early[at : at + BLOCK, :] = back[here, :]
            late[at : at + BLOCK, :] = branch[here, :]
    for k, out in enumerate(outs):
        cols = lanes(far ^ k, rows)
        out[:, : 2 * hidden] = tdot(normed[:, cols], gate_up_grad[...]).astype(bf16)
        out[:, 2 * hidden :] = tdot(mlp_grad[:, cols], activated[...]).astype(bf16)


def near_kernel(keep, got, out):
    half = 2 * BLOCK
    out[...] = (keep[half:, :].astype(f32) + got[half:, :].astype(f32)).astype(bf16)


def pair_kernel(keep, got, got_near, out):
    at = slice(BLOCK, 2 * BLOCK)
    out[...] = (keep[at, :].astype(f32) + got[at, :].astype(f32) + got_near[at, :].astype(f32)).astype(bf16)


def own_sum(keep, got, got_near, got_pair):
    terms = (got, got_near, got_pair)
    total = keep[:BLOCK, :].astype(f32)
    for term in terms:
        total = total + term[:BLOCK, :].astype(f32)
    return total


def onward_kernel(keep, got, out):
    out[...] = (keep[BLOCK:, :] + got[BLOCK:, :].astype(f32)).astype(bf16)


def middle_kernel(
    keep, got, got_near, got_pair, own_grad, residual, branch_one, scale_one, gain_two,
    residual_grad, attn_grad, rows,
):
    incoming = own_sum(keep, got, got_near, got_pair)
    grad = own_grad[...].astype(f32)
    unit, inverse = normalise(residual[...])
    scaled = incoming * gain_two[...]
    back = inverse * (
        scaled
        - jnp.mean(scaled, axis=1, keepdims=True)
        - unit * jnp.mean(scaled * unit, axis=1, keepdims=True)
    )
    total = grad + back
    residual_grad[...] = total
    attn_grad[...] = (scale_one[...] * total).astype(bf16)
    rows[...] = jnp.zeros(rows.shape, f32)
    rows[2:3, :] = jnp.sum(incoming * unit, axis=0, keepdims=True)
    rows[3:4, :] = jnp.sum(total * branch_one[...], axis=0, keepdims=True)


def finish_kernel(
    speaker, keep, got, got_near, got_pair, own_grad, residual, rows_in, scale_two, output, spread
):
    branch_two = own_sum(keep, got, got_near, got_pair)
    result = residual[...] + scale_two[...] * branch_two
    output[...] = result.astype(bf16)
    width = residual.shape[1]
    power = jnp.sum(result * result, axis=0, keepdims=True)
    scale_grad = jnp.sum(own_grad[...].astype(f32) * branch_two, axis=0, keepdims=True)
    for i in range(spread.shape[0]):
        spread[i, 0:1, :] = power
        spread[i, 1:2, :] = scale_grad
        spread[i, 2:4, :] = rows_in[2:4, :]
        spread[i, 4:5, :] = jnp.full((1, width), speaker[0], jnp.int32).astype(f32)


def attend_back_kernel(bounds, own, core, across, both, qkv, stat, cos, sin, *refs):
    outs, pieces, lefts, refs = refs[:4], refs[4 : 4 + PIECES], refs[4 + PIECES : 6 + PIECES], refs[6 + PIECES :]
    (keep, send), products, refs = refs[:2], refs[2 : 2 + PIECES], refs[2 + PIECES :]
    projected, weight, grads, att_grad, probs_all, score_all, parts, normed, attended, sems = refs
    wide, shard, first, second = wide_here(), shard_here(), bounds[0, 0], bounds[0, 1]
    group = parts.shape[2]
    out_copies = [
        pltpu.make_async_copy(outs[m].at[lanes(shard, group), :], parts.at[m], sems.at[m]) for m in range(4)
    ]
    copies = [
        pltpu.make_async_copy(
            pieces[j].at[:, pl.ds(0, 3 * group)], weight.at[lanes(feature_block(wide, j)), :], sems.at[4 + j]
        )
        for j in range(PIECES)
    ]
    copies += [
        pltpu.make_async_copy(left, here, sems.at[4 + PIECES + i])
        for i, (left, here) in enumerate(zip(lefts, (normed, attended)))
    ]
    for copy in out_copies + copies:
        copy.start()
    for b, x in enumerate((own, core, across, both)):
        grads[b * BLOCK : (b + 1) * BLOCK, :] = x[...]
    for copy in out_copies:
        copy.wait()
    tiles = group // BLOCK
    total = None
    for m in range(4):
        product = dot_t(grads[:, lanes(shard ^ m, group)], parts[m])
        total = product if total is None else total + product
    att_grad[...] = total.astype(bf16)
    keys = qkv.shape[0]
    scale = 64**-0.5
    for t in range(tiles):
        cols = slice(t * BLOCK, (t + 1) * BLOCK)
        key = qkv[:, group + t * BLOCK : group + (t + 1) * BLOCK]
        value = qkv[:, 2 * group + t * BLOCK : 2 * group + (t + 1) * BLOCK]
        query_grad = [None] * 4
        key_grad = None
        value_grad = None
        for h in range(2):
            for b in range(4):
                here = slice(b * BLOCK, (b + 1) * BLOCK)
                mask = allowed_pairs(shard, b, first, second, keys)
                query = qkv[here, cols]
                grad = att_grad[here, cols]
                keep_lanes = half_mask(h, query.shape)
                none = jnp.zeros_like(query)
                scores = dot_t(jnp.where(keep_lanes, query, none), key) * scale
                probs = jnp.where(mask, jnp.exp(scores - stat[here, 2 * t + h : 2 * t + h + 1]), 0.0)
                grad_here = jnp.where(keep_lanes, grad, none)
                prob_grad = dot_t(grad_here, value)
                delta = jnp.sum(probs * prob_grad, axis=1, keepdims=True)
                score_grad = (probs * (prob_grad - delta)).astype(bf16)
                probs_all[here, :] = probs.astype(bf16)
                score_all[here, :] = score_grad
                part = dot(score_grad, key)
                query_grad[b] = part if h == 0 else jnp.where(keep_lanes, part, query_grad[b])
            k_part = tdot(score_all[...], qkv[:, cols])
            v_part = tdot(probs_all[...], att_grad[:, cols])
            keep_all = half_mask(h, k_part.shape)
            key_grad = k_part if h == 0 else jnp.where(keep_all, k_part, key_grad)
            value_grad = v_part if h == 0 else jnp.where(keep_all, v_part, value_grad)
        for b in range(4):
            here = slice(b * BLOCK, (b + 1) * BLOCK)
            projected[here, cols] = turn(
                query_grad[b] * scale, cos[here, :], sin[here, :], -1.0
            ).astype(bf16)
        projected[:, group + t * BLOCK : group + (t + 1) * BLOCK] = turn(
            key_grad * scale, cos[...], sin[...], -1.0
        ).astype(bf16)
        projected[:, 2 * group + t * BLOCK : 2 * group + (t + 1) * BLOCK] = value_grad.astype(bf16)
    for copy in copies:
        copy.wait()
    for b, target in enumerate((keep, send, keep, send)):
        at = (b // 2) * BLOCK
        target[at : at + BLOCK, :] = dot_t(
            projected[b * BLOCK : (b + 1) * BLOCK, :], weight[...]
        ).astype(target.dtype)
    for j, out in enumerate(products):
        cols = lanes(feature_block(wide, j))
        out[:, : 3 * group] = tdot(normed[:, cols], projected[...]).astype(bf16)
        out[:, 3 * group :] = tdot(attended[:, cols], grads[:, lanes(shard, group)]).astype(bf16)


def last_kernel(keep, got_core, got_pair, frames, residual_grad, gain_one, frames_grad, spread):
    incoming = keep[:BLOCK, :] + got_core[:BLOCK, :].astype(f32) + got_pair[...].astype(f32)
    unit, inverse = normalise(frames[...].astype(f32))
    scaled = incoming * gain_one[...]
    back = inverse * (
        scaled
        - jnp.mean(scaled, axis=1, keepdims=True)
        - unit * jnp.mean(scaled * unit, axis=1, keepdims=True)
    )
    frames_grad[...] = (residual_grad[...] + back).astype(bf16)
    row = jnp.sum(incoming * unit, axis=0, keepdims=True)
    for i in range(spread.shape[0]):
        spread[i] = row


def copy_kernel(*refs):
    count = len(refs) // 2
    for source, target in zip(refs[:count], refs[count:]):
        target[...] = source[...]


def tick_kernel(out):
    out[...] = jnp.zeros(out.shape, f32)


def hops(x, count):
    def tick(after):
        return call(tick_kernel, "tick", [((8, BLOCK), f32)], [], after=[after])[0]

    small = tick(x)
    for _ in range(count):
        small = tick(swap(small, CORE))
    return small


def merge_kernel(terms, outs):
    total = terms[0][...].astype(f32)
    for term in terms[1:]:
        total = total + term[...].astype(f32)
    at = 0
    for out in outs:
        out[...] = total[:, at : at + out.shape[1]].astype(out.dtype)
        at += out.shape[1]


def merge(terms, outs, after=()):
    count = len(terms)
    return call(
        lambda *refs: merge_kernel(refs[:count], refs[count:]),
        "merge",
        [((terms[0].shape[0], width), dtype) for width, dtype in outs],
        terms,
        after=after,
    )


def split_rows_kernel(terms, outs):
    near = lax.axis_index(NEAR)
    rows = outs[0].shape[0]
    for out, whose in zip(outs, (near, 1 - near)):
        here = pl.ds(pl.multiple_of(whose * rows, rows), rows)
        total = terms[0][here, :].astype(f32)
        for term in terms[1:]:
            total = total + term[here, :].astype(f32)
        out[...] = total.astype(out.dtype)


def totals_kernel(rows, power, gain, one, two):
    count = rows.shape[0]
    ids = rows[:, 4, 0:1].astype(jnp.int32)
    lane = lax.broadcasted_iota(jnp.int32, (count, SPEAKERS), 1)
    one_hot = (lane == ids).astype(f32)

    def per_speaker(x):
        return lax.dot_general(
            one_hot, x, (((0,), (0,)), ((), ())), precision=highest, preferred_element_type=f32
        )

    sums = per_speaker(rows[:, 0, :])
    frames = per_speaker(jnp.full((count, BLOCK), float(BLOCK), f32))
    power[...] = sums / jnp.maximum(frames[:, 0:1], 1.0)
    two[...] = jnp.sum(rows[:, 1, :], axis=0, keepdims=True)
    gain[...] = jnp.sum(rows[:, 2, :], axis=0, keepdims=True)
    one[...] = jnp.sum(rows[:, 3, :], axis=0, keepdims=True)


def kernel_pieces(pieces):
    if len(pieces) == PIECES:
        return pieces
    ordered = from_pieces(jnp.concatenate(pieces, axis=0), 0)
    size = ordered.shape[0] // PIECES
    split = [ordered[b * size : (b + 1) * size] for b in range(PIECES)]
    return [split[(j % 4) * 2 + j // 4] for j in range(PIECES)]


def far_order(x):
    count = far_count()
    far = lax.axis_index(FAR)
    size = x.shape[0] // count
    return jnp.concatenate(
        [lax.dynamic_slice_in_dim(x, (far ^ k) * size, size, 0) for k in range(count)], axis=0
    )


def line_pieces(pieces):
    if len(pieces) == LINE:
        return pieces
    return jnp.split(far_order(jnp.concatenate(pieces, axis=0)), LINE, axis=0)


def slice_weights(sources, halves=1):
    rows = sources[0][0].shape[0]
    parts = []
    for x, count in sources:
        width = x.shape[1] // (4 * count * halves)
        parts.append(
            x.reshape(rows, count, 4, halves, width)
            .transpose(2, 0, 3, 1, 4)
            .reshape(4, rows, halves, count * width)
        )
    joined = jnp.concatenate(parts, axis=3)
    return joined.reshape(4, rows, halves * joined.shape[3])


def quarter_columns(x):
    near, pair = lax.axis_index(NEAR), lax.axis_index(PAIR)
    both = (NEAR, PAIR)
    across = [(i, 3 - i) for i in range(4)]

    def part(i, k):
        rows = lax.dynamic_index_in_dim(x, pair ^ i, 0, keepdims=False)
        return lax.dynamic_slice_in_dim(rows, (near ^ k) * (rows.shape[1] // 2), rows.shape[1] // 2, 1)

    came = {
        (0, 0): part(0, 0),
        (0, 1): swap(part(0, 1), NEAR),
        (1, 0): swap(part(1, 0), PAIR),
        (1, 1): lax.ppermute(part(1, 1), both, across),
    }
    by_near = [
        (jnp.where(near == 0, came[i, 0], came[i, 1]), jnp.where(near == 0, came[i, 1], came[i, 0]))
        for i in range(2)
    ]
    out = []
    for k in range(2):
        out.append(jnp.where(pair == 0, by_near[0][k], by_near[1][k]))
        out.append(jnp.where(pair == 0, by_near[1][k], by_near[0][k]))
    return jnp.concatenate(out, axis=0)


def sum_wide(own, other, outs):
    if far_count() != LINE:
        return sum_wide_long(own, other, outs), []
    whole = [(own[0].shape[1], bf16)]
    near = [swap(x, NEAR) for x in other]
    third = merge([own[3], near[3]], whole)
    halfway = merge([own[2], near[2], swap_far(third[0], 1)], whole)[0]
    first = merge([own[1], near[1]], whole, third)[0]
    return merge([own[0], near[0], swap_far(first, 1), swap_far(halfway, 2)], outs), third


def sum_wide_long(own, other, outs):
    count = far_count()
    ordered = [(own + other)[(b % 2) * 4 + b // 2] for b in range(PIECES)]
    pieces = to_pieces(jnp.concatenate([x.astype(f32) for x in ordered], axis=0), 0)
    size = pieces.shape[0] // (2 * count)
    parts = {}
    for i in range(2):
        for k in range(count):
            at = (i * count + k) * size
            parts[i, k] = pieces[at : at + size]
    total = scatter_parts(parts)
    at = 0
    result = []
    for width, dtype in outs:
        result.append(total[:, at : at + width].astype(dtype))
        at += width
    return result


def split_rows(terms, after):
    rows, width = terms[0].shape
    if rows % 32 != 0:
        near = lax.axis_index(NEAR)
        total = sum(x.astype(f32) for x in terms).reshape(2, rows // 2, width)
        return (
            lax.dynamic_index_in_dim(total, near, 0, keepdims=False),
            lax.dynamic_index_in_dim(total, 1 - near, 0, keepdims=False).astype(bf16),
        )
    return call(
        lambda *refs: split_rows_kernel(refs[: len(terms)], refs[len(terms) :]),
        "merge",
        [((rows // 2, width), f32), ((rows // 2, width), bf16)],
        terms,
        after=after,
    )


def sum_line(parts):
    count = far_count()
    pieces = jnp.split(far_order(jnp.concatenate(parts, axis=0).astype(f32)), count, axis=0)
    for j in range(count - 1, 0, -1):
        low = j & -j
        pieces[j ^ low] = pieces[j ^ low] + swap_far(pieces[j].astype(bf16), low).astype(f32)
    return pieces[0]


def body(
    frames,
    out_grad,
    qkv_weight,
    out_weight,
    gate_up_weight,
    down_weight_t,
    norm_gain_one,
    norm_gain_two,
    layer_scale_one,
    layer_scale_two,
    speaker,
    clip_bounds,
):
    streams, shard_len, width = frames.shape
    pair = lax.axis_index(PAIR)
    core = lax.axis_index(CORE)
    near = lax.axis_index(NEAR)
    shard = pair * 2 + core
    group = width // 4
    hidden = gate_up_weight.shape[1] // 16
    head_size = width // HEADS
    tokens = 4 * shard_len

    slice_a = pair_columns(core_columns(slice_weights([(qkv_weight, 3), (out_weight, 1)])))
    slice_b = quarter_columns(core_columns(slice_weights([(gate_up_weight, 2), (down_weight_t, 1)], halves=2)))
    pieces_a = kernel_pieces(gather_rows(slice_a))
    line_b = gather_line(slice_b)
    pieces_b = line_pieces(line_b)

    bounds = clip_bounds.astype(jnp.int32)
    gain_one = norm_gain_one[None]
    gain_two = norm_gain_two[None]
    scale_one = layer_scale_one[None]
    scale_two = layer_scale_two[None]
    frames_here, grad_here = call(
        copy_kernel,
        "fence",
        [((shard_len, width), bf16)] * 2,
        [frames.reshape(shard_len, width), out_grad.reshape(shard_len, width)],
        after=[slice_a],
    )

    def spread(x):
        across = swap(x, PAIR)
        return x, swap(x, CORE), across, swap(across, CORE)

    frames_all = spread(frames_here)
    grad_all = (*spread(grad_here), *spread(swap(grad_here, NEAR)))

    block = shard ^ jnp.arange(4, dtype=jnp.int32)
    positions = (block[:, None] * shard_len + jnp.arange(shard_len, dtype=jnp.int32)[None]).reshape(-1)
    half_size = head_size // 2
    lane = jnp.arange(BLOCK, dtype=jnp.int32)
    inverse_freq = jnp.exp((lane % half_size).astype(f32) * (-math.log(10000.0) / half_size))
    angles = positions.astype(f32)[:, None] * inverse_freq[None, :]
    cosine = jnp.cos(angles)
    sine = jnp.where(lane % head_size < half_size, -1.0, 1.0)[None, :] * jnp.sin(angles)

    (out_own,) = call(
        out_kernel,
        "out",
        [((width, group), bf16)],
        pieces_a,
        [pltpu.SemaphoreType.DMA((PIECES,))],
        anywhere=range(PIECES),
    )
    normed_one, qkv, stat, att, att_to_core, att_to_pair = call(
        attend_kernel,
        "attend",
        [
            ((tokens, width), bf16),
            ((tokens, 3 * group), bf16),
            ((tokens, BLOCK), f32),
            ((tokens, group), bf16),
            ((tokens, group), bf16),
            ((tokens, group), bf16),
        ],
        [bounds, *frames_all, *pieces_a, gain_one, cosine, sine],
        [pltpu.VMEM((width, 3 * group), bf16), pltpu.SemaphoreType.DMA((PIECES,))],
        smem=1,
        anywhere=range(5, 5 + PIECES),
        megabytes=52,
        after=[line_b[1], line_b[2], out_own],
    )
    att_pair = swap(att_to_pair, PAIR)
    att_core = swap(att_to_core, CORE)
    att_both = swap(att_pair, CORE)
    out_pair = swap(out_own, PAIR)
    outs = (out_own, swap(out_own, CORE), out_pair, swap(out_pair, CORE))

    normed_here, normed_even, attended, residual, branch_one = call(
        residual_kernel,
        "residual",
        [
            ((tokens, width), bf16),
            ((tokens // 2, width), bf16),
            ((tokens, width), bf16),
            ((shard_len, width), f32),
            ((shard_len, width), f32),
        ],
        [*frames_all, att, att_core, att_pair, att_both, *outs, scale_one, gain_two],
        [pltpu.VMEM((tokens, width), f32)],
        megabytes=52,
        after=[line_b[1], line_b[3], *grad_all],
    )

    near_even = swap(normed_even, NEAR)
    near_odd = swap(near_even, CORE)
    rows_b = width // LINE
    keep, send, keep_late, send_late, *grads_b = call(
        mlp_kernel,
        "mlp",
        [((tokens, width), bf16)] * 4 + [((rows_b, 3 * hidden), bf16)] * LINE,
        [normed_here, near_even, near_odd, *grad_all, *pieces_b, scale_two],
        [
            pltpu.VMEM((2 * tokens, width), bf16),
            pltpu.VMEM((2 * tokens, width), bf16),
            pltpu.VMEM((2 * tokens, hidden), bf16),
            pltpu.VMEM((2 * tokens, 2 * hidden), bf16),
            pltpu.VMEM((width, 3 * hidden), bf16),
            pltpu.SemaphoreType.DMA((LINE,)),
        ],
        anywhere=range(11, 11 + LINE),
        megabytes=52,
    )

    half_shape = ((2 * shard_len, width), bf16)
    own_shape = ((shard_len, width), bf16)

    got = swap(send, CORE)
    to_near = call(near_kernel, "onward", [half_shape], [keep, got])[0]
    got_near = swap(to_near, NEAR)
    got_late = swap(send_late, CORE)
    to_near_late = call(near_kernel, "onward", [half_shape], [keep_late, got_late], after=[to_near])[0]
    to_pair = call(pair_kernel, "onward", [own_shape], [keep, got, got_near], after=[to_near_late])[0]
    near_late = swap(to_near_late, NEAR)
    residual_grad, attn_grad, rows = call(
        middle_kernel,
        "middle",
        [((shard_len, width), f32), ((shard_len, width), bf16), ((8, width), f32)],
        [keep, got, got_near, swap(to_pair, PAIR), grad_here, residual, branch_one, scale_one, gain_two],
    )
    to_pair_late = call(
        pair_kernel, "onward", [own_shape], [keep_late, got_late, near_late], after=[attn_grad]
    )[0]
    met_late = (keep_late, got_late, near_late, swap(to_pair_late, PAIR))
    if far_count() == LINE:
        third_b, first_b = swap_far(grads_b[3], 1), swap_far(grads_b[1], 1)
        halfway_b = merge([grads_b[2], third_b], [(3 * hidden, bf16)], [attn_grad])[0]
        terms_b = [grads_b[0], first_b, swap_far(halfway_b, 2)]
    else:
        halfway_b = sum_line(grads_b)
        terms_b = [halfway_b]
    keep, send, *grads_a = call(
        attend_back_kernel,
        "attend_back",
        [((2 * shard_len, width), f32), ((2 * shard_len, width), bf16)]
        + [((BLOCK, 4 * group), bf16)] * PIECES,
        [bounds, *spread(attn_grad), qkv, stat, cosine, sine, *outs, *pieces_a, normed_one, attended],
        [
            pltpu.VMEM((tokens, 3 * group), bf16),
            pltpu.VMEM((width, 3 * group), bf16),
            pltpu.VMEM((tokens, width), bf16),
            pltpu.VMEM((tokens, group), bf16),
            pltpu.VMEM((tokens, tokens), bf16),
            pltpu.VMEM((tokens, tokens), bf16),
            pltpu.VMEM((4, group, group), bf16),
            pltpu.VMEM((tokens, width), bf16),
            pltpu.VMEM((tokens, width), bf16),
            pltpu.SemaphoreType.DMA((6 + PIECES,)),
        ],
        smem=1,
        anywhere=range(9, 15 + PIECES),
        megabytes=24,
        after=[to_pair_late, halfway_b],
    )
    own_a, other_a = grads_a[:4], grads_a[4:]
    got = swap(send, CORE)
    onward = call(onward_kernel, "onward", [((shard_len, width), bf16)], [keep, got])[0]
    output, early_spread = call(
        finish_kernel,
        "finish",
        [((shard_len, width), bf16), ((far_count() * 8, 5, width), f32)],
        [speaker.astype(jnp.int32), *met_late, grad_here, residual, rows, scale_two],
        smem=1,
        after=[onward],
    )
    (query_sum, key_sum, value_sum, out_sum), third_a = sum_wide(
        own_a, other_a, [(group, bf16)] * 3 + [(group, f32)]
    )
    kept_b, left_b = split_rows(terms_b, third_a)
    came_b = swap(left_b, NEAR)
    def everywhere(vectors):
        return lax.all_to_all(vectors, ALL, 0, 0, tiled=True)

    early = everywhere(early_spread)
    frames_grad, late_spread = call(
        last_kernel,
        "last",
        [((shard_len, width), bf16), ((far_count() * 8, 1, width), f32)],
        [keep, got, swap(onward, PAIR), frames_here, residual_grad, gain_one],
        after=(),
    )
    late = everywhere(late_spread)
    speaker_power, gain_two_grad, scale_one_grad, scale_two_grad = call(
        totals_kernel, "totals", [((SPEAKERS, width), f32)] + [((1, width), f32)] * 3, [early]
    )

    def near_order(kept, came):
        return jnp.concatenate(
            [jnp.where(near == 0, kept, came), jnp.where(near == 0, came, kept)], axis=1
        )

    kept_low = kept_b[:, : 2 * hidden].astype(bf16)
    gate_up_grad_out = place_gate_up(
        near_order(kept_low[:, :hidden], came_b[:, :hidden]),
        near_order(kept_low[:, hidden:], came_b[:, hidden : 2 * hidden]),
        pair,
        core,
    )
    down_grad = near_order(kept_b[:, 2 * hidden :], came_b[:, 2 * hidden :].astype(f32))
    qkv_grad_out = place_qkv(query_sum, key_sum, value_sum, pair, core)
    return (
        output.reshape(frames.shape),
        speaker_power,
        frames_grad.reshape(frames.shape),
        qkv_grad_out,
        out_sum,
        gate_up_grad_out,
        down_grad,
        jnp.sum(late[:, 0], axis=0),
        gain_two_grad[0],
        scale_one_grad[0],
        scale_two_grad[0],
    )


def place_gate_up(gate, up, pair, core):
    narrow = (PAIR, CORE)
    shard = pair * 2 + core
    first = jnp.where(shard == 1, up, gate)
    second = jnp.where(shard == 0, up, gate)
    second = jnp.where(shard == 2, up, second)
    got_one = lax.ppermute(first, narrow, [(1, 2), (2, 1)])
    got_two = lax.ppermute(second, narrow, [(0, 2), (1, 0), (2, 3), (3, 1)])
    left = jnp.where(shard == 0, gate, jnp.where(shard == 1, got_one, got_two))
    right = jnp.where(shard == 3, up, jnp.where(shard == 2, got_one, got_two))
    return jnp.concatenate([left, right], axis=1).astype(f32)


def place_qkv(query, key, value, pair, core):
    shard = pair * 2 + core
    to_core = jnp.where(
        shard == 0, key, jnp.where(shard == 1, query, jnp.where(shard == 2, value, key))
    )
    to_pair = jnp.where(pair == 0, value, query)
    stay = jnp.where(shard == 0, query, jnp.where(shard == 3, value, key))
    got_core = swap(to_core, CORE)
    got_pair = swap(to_pair, PAIR)
    left = jnp.where(core == 0, stay, got_pair)
    right = jnp.where(core == 0, got_pair, stay)
    return jnp.concatenate([left, got_core, right], axis=1).astype(f32)


def solution(mesh):
    wide = mesh.shape["wide"]
    split = Mesh(mesh.devices.reshape(wide // 2, 2, 2, 2), ALL)
    both = (FAR, NEAR)
    narrow = (PAIR, CORE)
    placed = (
        P(both, narrow, None),
        P(both, narrow, None),
        P(ALL, None),
        P(ALL, None),
        P(ALL, None),
        P(ALL, None),
        P(),
        P(),
        P(),
        P(),
        P(both),
        P(both, None),
    )
    return jax.shard_map(
        body,
        mesh=split,
        in_specs=placed,
        out_specs=(
            P(both, narrow, None),
            P(),
            P(both, narrow, None),
            P(both, narrow),
            P(both, narrow),
            P(both, narrow),
            P(both, narrow),
            P(),
            P(),
            P(),
            P(),
        ),
        check_vma=False,
    )
```

```python
import functools
import math

import jax
import jax.numpy as jnp
from jax import lax
from jax.experimental import pallas as pl
from jax.experimental.pallas import tpu as pltpu
from jax.sharding import Mesh, PartitionSpec as P

HEADS = 16
WINDOW = 128
CLIP_LEN = 512
SPEAKERS = 128

bf16 = jnp.bfloat16
f32 = jnp.float32
highest = lax.Precision.HIGHEST

FAR, NEAR, PAIR, CORE = "far", "near", "pair", "core"
ALL = (FAR, NEAR, PAIR, CORE)
SWAP = [(0, 1), (1, 0)]


def swap(x, axis):
    return lax.ppermute(x, axis, SWAP)


def dot(a, b):
    return jnp.dot(a, b, preferred_element_type=f32)


def dot_t(a, b):
    return lax.dot_general(a, b, (((1,), (1,)), ((), ())), preferred_element_type=f32)


def tdot(a, b):
    return lax.dot_general(a, b, (((0,), (0,)), ((), ())), preferred_element_type=f32)


def far_count():
    return lax.axis_size(FAR)


def piece_index():
    far, near = lax.axis_index(FAR), lax.axis_index(NEAR)
    return [(far ^ k) * 2 + (near ^ i) for i in range(2) for k in range(far_count())]


def to_pieces(x, axis):
    size = x.shape[axis] // (2 * far_count())
    return jnp.concatenate(
        [lax.dynamic_slice_in_dim(x, i * size, size, axis) for i in piece_index()], axis=axis
    )


def from_pieces(x, axis):
    count = far_count()
    far, near = lax.axis_index(FAR), lax.axis_index(NEAR)
    size = x.shape[axis] // (2 * count)
    return jnp.concatenate(
        [
            lax.dynamic_slice_in_dim(x, ((near ^ i) * count + (far ^ k)) * size, size, axis)
            for k in range(count)
            for i in range(2)
        ],
        axis=axis,
    )


def swap_far(x, bit):
    return lax.ppermute(x, FAR, [(i, i ^ bit) for i in range(far_count())])


def gather_line(block):
    own = [block]
    for j in range(1, far_count()):
        low = j & -j
        own.append(swap_far(own[j ^ low], low))
    return own


def gather_rows(block):
    own = gather_line(block)
    return own + [swap(x, NEAR) for x in own]


def scatter_parts(parts):
    count = far_count()
    total = [
        parts[0, k] + swap(parts[1, k].astype(bf16), NEAR).astype(f32) for k in range(count)
    ]
    for j in range(count - 1, 0, -1):
        low = j & -j
        total[j ^ low] = total[j ^ low] + swap_far(total[j].astype(bf16), low).astype(f32)
    return total[0]


def core_columns(x):
    core = lax.axis_index(CORE)
    slices = [[x[0], x[1]], [x[2], x[3]]]
    stay = jnp.stack([jnp.where(core == 0, s[0], s[1]) for s in slices])
    send = jnp.stack([jnp.where(core == 0, s[1], s[0]) for s in slices])
    got = swap(send, CORE)
    return jnp.concatenate([jnp.where(core == 0, stay, got), jnp.where(core == 0, got, stay)], axis=1)


def pair_columns(x):
    pair = lax.axis_index(PAIR)
    stay = jnp.where(pair == 0, x[0], x[1])
    got = swap(jnp.where(pair == 0, x[1], x[0]), PAIR)
    return jnp.concatenate([jnp.where(pair == 0, stay, got), jnp.where(pair == 0, got, stay)], axis=0)


BLOCK = 128
PIECES = 8
LINE = 4
ROWS = 6
MICROSECONDS = dict(
    attend=9, residual=3, mlp=11, middle=2, finish=2, attend_back=11, last=2, rows=1, onward=1, merge=1, weight_grad=2,
    fence=1, tick=0, totals=1, out=0,
)
RATE = 10**8


def call(kernel, name, outs, ins, scratch=(), smem=0, anywhere=(), far_outs=(), megabytes=24, after=()):
    specs = []
    given = len(ins)
    if len(after) > 0:
        inner = kernel

        def kernel(*refs):
            inner(*refs[:given], *refs[given + len(after) :])

    for i in range(len(ins)):
        if i < smem:
            specs.append(pl.BlockSpec(memory_space=pltpu.SMEM))
        elif i in anywhere:
            specs.append(pl.BlockSpec(memory_space=pltpu.HBM))
        else:
            specs.append(pl.BlockSpec(memory_space=pltpu.VMEM))
    specs += [pl.BlockSpec(memory_space=pl.ANY)] * len(after)
    return pl.pallas_call(
        kernel,
        out_shape=[jax.ShapeDtypeStruct(shape, dtype) for shape, dtype in outs],
        in_specs=specs,
        out_specs=[
            pl.BlockSpec(memory_space=pltpu.HBM if i in far_outs else pltpu.VMEM) for i in range(len(outs))
        ],
        scratch_shapes=list(scratch),
        compiler_params=pltpu.CompilerParams(vmem_limit_bytes=megabytes * 2**20),
        cost_estimate=pl.CostEstimate(
            flops=int(MICROSECONDS[name] * RATE), bytes_accessed=0, transcendentals=0
        ),
        name=name,
    )(*ins, *after)


def wide_here():
    if lax.axis_size(FAR) != LINE:
        return 0
    return lax.axis_index(FAR) * 2 + lax.axis_index(NEAR)


def far_here():
    return lax.axis_index(FAR) if lax.axis_size(FAR) == LINE else 0


def shard_here():
    return lax.axis_index(PAIR) * 2 + lax.axis_index(CORE)


def feature_block(wide, piece):
    return wide ^ ((piece % 4) * 2 + piece // 4)


def lanes(block, size=BLOCK):
    return pl.ds(pl.multiple_of(block * size, size), size)


def normalise(x):
    centred = x - jnp.mean(x, axis=1, keepdims=True)
    inverse = lax.rsqrt(jnp.mean(centred * centred, axis=1, keepdims=True) + 1e-05)
    return centred * inverse, inverse


def turn(x, cos, sin, sign):
    lane = lax.broadcasted_iota(jnp.int32, x.shape, 1)
    lower = (lane & 63) < 32
    partner = jnp.where(lower, pltpu.roll(x, BLOCK - 32, 1), pltpu.roll(x, 32, 1))
    return x * cos + (sign * partner) * sin


def allowed_pairs(shard, block, first, second, keys):
    row = lax.broadcasted_iota(jnp.int32, (BLOCK, keys), 0)
    lane = lax.broadcasted_iota(jnp.int32, (BLOCK, keys), 1)
    query = (shard ^ block) * BLOCK + row
    key = (shard ^ (lane // BLOCK)) * BLOCK + lane % BLOCK

    def segment(position):
        return (position >= first).astype(jnp.int32) + (position >= second).astype(jnp.int32)

    return (jnp.abs(query - key) <= WINDOW) & (segment(query) == segment(key))


def half_mask(head, shape):
    lane = lax.broadcasted_iota(jnp.int32, shape, 1)
    return (lane // 64) == head


def out_kernel(*refs):
    pieces, (out, sems) = refs[:PIECES], refs[PIECES:]
    group = out.shape[1]
    copies = [
        pltpu.make_async_copy(
            pieces[j].at[:, pl.ds(3 * group, group)],
            out.at[lanes(feature_block(wide_here(), j)), :],
            sems.at[j],
        )
        for j in range(PIECES)
    ]
    for copy in copies:
        copy.start()
    for copy in copies:
        copy.wait()


def attend_kernel(bounds, own, core, across, both, *refs):
    pieces = refs[:PIECES]
    gain, cos, sin, normed, qkv, stat, att, att_core, att_pair, weight, sems = refs[PIECES:]
    wide, shard, first, second = wide_here(), shard_here(), bounds[0, 0], bounds[0, 1]
    group = att.shape[1]
    copies = [
        pltpu.make_async_copy(
            pieces[j].at[:, pl.ds(0, 3 * group)], weight.at[lanes(feature_block(wide, j)), :], sems.at[j]
        )
        for j in range(PIECES)
    ]
    for copy in copies:
        copy.start()
    for b, x in enumerate((own, core, across, both)):
        unit, _ = normalise(x[...].astype(f32))
        normed[b * BLOCK : (b + 1) * BLOCK, :] = (unit * gain[...]).astype(bf16)
    for copy in copies:
        copy.wait()
    tiles = group // BLOCK
    for part in range(3):
        x = dot(normed[...], weight[:, part * group : (part + 1) * group])
        for t in range(tiles):
            y = x[:, t * BLOCK : (t + 1) * BLOCK]
            if part < 2:
                y = turn(y, cos[...], sin[...], 1.0)
            at = part * group + t * BLOCK
            qkv[:, at : at + BLOCK] = y.astype(bf16)
    keys = normed.shape[0]
    scale = 64**-0.5
    for b in range(4):
        here = slice(b * BLOCK, (b + 1) * BLOCK)
        mask = allowed_pairs(shard, b, first, second, keys)
        stats = jnp.zeros((BLOCK, BLOCK), f32)
        for t in range(tiles):
            query = qkv[here, t * BLOCK : (t + 1) * BLOCK]
            key = qkv[:, group + t * BLOCK : group + (t + 1) * BLOCK]
            value = qkv[:, 2 * group + t * BLOCK : 2 * group + (t + 1) * BLOCK]
            merged = None
            for h in range(2):
                keep = half_mask(h, query.shape)
                scores = dot_t(jnp.where(keep, query, jnp.zeros_like(query)), key) * scale
                scores = jnp.where(mask, scores, -1e30)
                peak = jnp.max(scores, axis=1, keepdims=True)
                exponent = jnp.exp(scores - peak)
                total = jnp.sum(exponent, axis=1, keepdims=True)
                probs = (exponent * (1.0 / total)).astype(bf16)
                lane = lax.broadcasted_iota(jnp.int32, stats.shape, 1)
                stats = jnp.where(lane == 2 * t + h, peak + jnp.log(total), stats)
                part = dot(probs, value)
                merged = part if merged is None else jnp.where(keep, part, merged)
            merged = merged.astype(bf16)
            cols = slice(t * BLOCK, (t + 1) * BLOCK)
            att[here, cols] = merged
            to_core, to_pair = b ^ 1, b ^ 2
            att_core[to_core * BLOCK : (to_core + 1) * BLOCK, cols] = merged
            att_pair[to_pair * BLOCK : (to_pair + 1) * BLOCK, cols] = merged
        stat[here, :] = stats


def residual_kernel(
    own, core, across, both, att0, att1, att2, att3, out0, out1, out2, out3, scale_one, gain_two,
    normed, normed_even, attended, residual_own, branch_own, branch,
):
    shard = shard_here()
    group = out0.shape[1]
    for m, part in enumerate((att0, att1)):
        attended[:, lanes(shard ^ m, group)] = part[...]
    attended[:, lanes(shard ^ 2, group)] = att2[...]
    for b in range(4):
        attended[b * BLOCK : (b + 1) * BLOCK, lanes(shard ^ 3, group)] = att3[
            (b ^ 1) * BLOCK : ((b ^ 1) + 1) * BLOCK, :
        ]
    for m, part in enumerate((out0, out1, out2, out3)):
        branch[:, lanes(shard ^ m, group)] = dot(attended[...], part[...])
    for b, x in enumerate((own, core, across, both)):
        here = slice(b * BLOCK, (b + 1) * BLOCK)
        total = x[...].astype(f32) + scale_one[...] * branch[here, :]
        unit, _ = normalise(total)
        low = (unit * gain_two[...]).astype(bf16)
        normed[here, :] = low
        if b % 2 == 0:
            normed_even[b // 2 * BLOCK : (b // 2 + 1) * BLOCK, :] = low
        if b == 0:
            residual_own[...] = total
            branch_own[...] = branch[here, :]


def mlp_kernel(normed_here, near_even, near_odd, *refs):
    grads, refs = refs[:8], refs[8:]
    pieces, scale_two, refs = refs[:LINE], refs[LINE], refs[LINE + 1 :]
    (keep, send, keep_late, send_late), outs, refs = refs[:4], refs[4 : 4 + LINE], refs[4 + LINE :]
    normed, mlp_grad, activated, gate_up_grad, weight, sems = refs
    far = far_here()
    rows = pieces[0].shape[0]
    copies = [
        pltpu.make_async_copy(pieces[k], weight.at[lanes(far ^ k, rows), :], sems.at[k]) for k in range(LINE)
    ]
    for copy in copies:
        copy.start()
    tokens = 4 * BLOCK
    normed[:tokens, :] = normed_here[...]
    for b in range(4):
        source = near_odd if b % 2 else near_even
        normed[tokens + b * BLOCK : tokens + (b + 1) * BLOCK, :] = source[b // 2 * BLOCK : (b // 2 + 1) * BLOCK, :]
    for b, x in enumerate(grads):
        mlp_grad[b * BLOCK : (b + 1) * BLOCK, :] = (scale_two[...] * x[...].astype(f32)).astype(bf16)
    for copy in copies:
        copy.wait()
    hidden = activated.shape[1]
    gate_at, up_at, down_at = [slice(i * hidden, (i + 1) * hidden) for i in range(3)]
    for stream in range(2):
        here = slice(stream * tokens, (stream + 1) * tokens)
        gate = dot(normed[here, :], weight[:, gate_at])
        up = dot(normed[here, :], weight[:, up_at])
        act_grad = dot(mlp_grad[here, :], weight[:, down_at])
        sigmoid = 1.0 / (1.0 + jnp.exp(-gate))
        silu = gate * sigmoid
        activated[here, :] = (silu * up).astype(bf16)
        gate_up_grad[here, gate_at] = (act_grad * up * sigmoid * (1.0 + gate * (1.0 - sigmoid))).astype(bf16)
        gate_up_grad[here, up_at] = (act_grad * silu).astype(bf16)
        back = dot_t(gate_up_grad[here, gate_at], weight[:, gate_at])
        back = (back + dot_t(gate_up_grad[here, up_at], weight[:, up_at])).astype(bf16)
        branch = dot_t(activated[here, :], weight[:, down_at]).astype(bf16)
        for b in range(4):
            here = slice(b * BLOCK, (b + 1) * BLOCK)
            at = stream * 2 * BLOCK + b // 2 * BLOCK
            early, late = (send, send_late) if b % 2 else (keep, keep_late)
            early[at : at + BLOCK, :] = back[here, :]
            late[at : at + BLOCK, :] = branch[here, :]
    for k, out in enumerate(outs):
        cols = lanes(far ^ k, rows)
        out[:, : 2 * hidden] = tdot(normed[:, cols], gate_up_grad[...]).astype(bf16)
        out[:, 2 * hidden :] = tdot(mlp_grad[:, cols], activated[...]).astype(bf16)


def near_kernel(keep, got, out):
    half = 2 * BLOCK
    out[...] = (keep[half:, :].astype(f32) + got[half:, :].astype(f32)).astype(bf16)


def pair_kernel(keep, got, got_near, out):
    at = slice(BLOCK, 2 * BLOCK)
    out[...] = (keep[at, :].astype(f32) + got[at, :].astype(f32) + got_near[at, :].astype(f32)).astype(bf16)


def own_sum(keep, got, got_near, got_pair):
    terms = (got, got_near, got_pair)
    total = keep[:BLOCK, :].astype(f32)
    for term in terms:
        total = total + term[:BLOCK, :].astype(f32)
    return total


def onward_kernel(keep, got, out):
    out[...] = (keep[BLOCK:, :] + got[BLOCK:, :].astype(f32)).astype(bf16)


def middle_kernel(
    keep, got, got_near, got_pair, own_grad, residual, branch_one, scale_one, gain_two,
    residual_grad, attn_grad, rows,
):
    incoming = own_sum(keep, got, got_near, got_pair)
    grad = own_grad[...].astype(f32)
    unit, inverse = normalise(residual[...])
    scaled = incoming * gain_two[...]
    back = inverse * (
        scaled
        - jnp.mean(scaled, axis=1, keepdims=True)
        - unit * jnp.mean(scaled * unit, axis=1, keepdims=True)
    )
    total = grad + back
    residual_grad[...] = total
    attn_grad[...] = (scale_one[...] * total).astype(bf16)
    rows[...] = jnp.zeros(rows.shape, f32)
    rows[2:3, :] = jnp.sum(incoming * unit, axis=0, keepdims=True)
    rows[3:4, :] = jnp.sum(total * branch_one[...], axis=0, keepdims=True)


def finish_kernel(speaker, keep, got, got_near, got_pair, own_grad, residual, rows_in, scale_two, output, rows):
    branch_two = own_sum(keep, got, got_near, got_pair)
    result = residual[...] + scale_two[...] * branch_two
    output[...] = result.astype(bf16)
    rows[0:1, :] = jnp.sum(result * result, axis=0, keepdims=True)
    rows[1:2, :] = jnp.sum(own_grad[...].astype(f32) * branch_two, axis=0, keepdims=True)
    rows[2:4, :] = rows_in[2:4, :]
    rows[4:5, :] = jnp.full((1, residual.shape[1]), speaker[0], jnp.int32).astype(f32)
    rows[5:8, :] = jnp.zeros((3, residual.shape[1]), f32)


def attend_back_kernel(bounds, own, core, across, both, qkv, stat, cos, sin, *refs):
    outs, pieces, lefts, refs = refs[:4], refs[4 : 4 + PIECES], refs[4 + PIECES : 6 + PIECES], refs[6 + PIECES :]
    (keep, send), products, refs = refs[:2], refs[2 : 2 + PIECES], refs[2 + PIECES :]
    projected, weight, grads, att_grad, probs_all, score_all, parts, normed, attended, sems = refs
    wide, shard, first, second = wide_here(), shard_here(), bounds[0, 0], bounds[0, 1]
    group = parts.shape[2]
    out_copies = [
        pltpu.make_async_copy(outs[m].at[lanes(shard, group), :], parts.at[m], sems.at[m]) for m in range(4)
    ]
    copies = [
        pltpu.make_async_copy(
            pieces[j].at[:, pl.ds(0, 3 * group)], weight.at[lanes(feature_block(wide, j)), :], sems.at[4 + j]
        )
        for j in range(PIECES)
    ]
    copies += [
        pltpu.make_async_copy(left, here, sems.at[4 + PIECES + i])
        for i, (left, here) in enumerate(zip(lefts, (normed, attended)))
    ]
    for copy in out_copies + copies:
        copy.start()
    for b, x in enumerate((own, core, across, both)):
        grads[b * BLOCK : (b + 1) * BLOCK, :] = x[...]
    for copy in out_copies:
        copy.wait()
    tiles = group // BLOCK
    total = None
    for m in range(4):
        product = dot_t(grads[:, lanes(shard ^ m, group)], parts[m])
        total = product if total is None else total + product
    att_grad[...] = total.astype(bf16)
    keys = qkv.shape[0]
    scale = 64**-0.5
    for t in range(tiles):
        cols = slice(t * BLOCK, (t + 1) * BLOCK)
        key = qkv[:, group + t * BLOCK : group + (t + 1) * BLOCK]
        value = qkv[:, 2 * group + t * BLOCK : 2 * group + (t + 1) * BLOCK]
        query_grad = [None] * 4
        key_grad = None
        value_grad = None
        for h in range(2):
            for b in range(4):
                here = slice(b * BLOCK, (b + 1) * BLOCK)
                mask = allowed_pairs(shard, b, first, second, keys)
                query = qkv[here, cols]
                grad = att_grad[here, cols]
                keep_lanes = half_mask(h, query.shape)
                none = jnp.zeros_like(query)
                scores = dot_t(jnp.where(keep_lanes, query, none), key) * scale
                probs = jnp.where(mask, jnp.exp(scores - stat[here, 2 * t + h : 2 * t + h + 1]), 0.0)
                grad_here = jnp.where(keep_lanes, grad, none)
                prob_grad = dot_t(grad_here, value)
                delta = jnp.sum(probs * prob_grad, axis=1, keepdims=True)
                score_grad = (probs * (prob_grad - delta)).astype(bf16)
                probs_all[here, :] = probs.astype(bf16)
                score_all[here, :] = score_grad
                part = dot(score_grad, key)
                query_grad[b] = part if h == 0 else jnp.where(keep_lanes, part, query_grad[b])
            k_part = tdot(score_all[...], qkv[:, cols])
            v_part = tdot(probs_all[...], att_grad[:, cols])
            keep_all = half_mask(h, k_part.shape)
            key_grad = k_part if h == 0 else jnp.where(keep_all, k_part, key_grad)
            value_grad = v_part if h == 0 else jnp.where(keep_all, v_part, value_grad)
        for b in range(4):
            here = slice(b * BLOCK, (b + 1) * BLOCK)
            projected[here, cols] = turn(
                query_grad[b] * scale, cos[here, :], sin[here, :], -1.0
            ).astype(bf16)
        projected[:, group + t * BLOCK : group + (t + 1) * BLOCK] = turn(
            key_grad * scale, cos[...], sin[...], -1.0
        ).astype(bf16)
        projected[:, 2 * group + t * BLOCK : 2 * group + (t + 1) * BLOCK] = value_grad.astype(bf16)
    for copy in copies:
        copy.wait()
    for b, target in enumerate((keep, send, keep, send)):
        at = (b // 2) * BLOCK
        target[at : at + BLOCK, :] = dot_t(
            projected[b * BLOCK : (b + 1) * BLOCK, :], weight[...]
        ).astype(target.dtype)
    for j, out in enumerate(products):
        cols = lanes(feature_block(wide, j))
        out[:, : 3 * group] = tdot(normed[:, cols], projected[...]).astype(bf16)
        out[:, 3 * group :] = tdot(attended[:, cols], grads[:, lanes(shard, group)]).astype(bf16)


def last_kernel(keep, got_core, got_pair, frames, residual_grad, gain_one, rows, frames_grad, spread, block):
    incoming = keep[:BLOCK, :] + got_core[:BLOCK, :].astype(f32) + got_pair[...].astype(f32)
    unit, inverse = normalise(frames[...].astype(f32))
    scaled = incoming * gain_one[...]
    back = inverse * (
        scaled
        - jnp.mean(scaled, axis=1, keepdims=True)
        - unit * jnp.mean(scaled * unit, axis=1, keepdims=True)
    )
    frames_grad[...] = (residual_grad[...] + back).astype(bf16)
    row = jnp.sum(incoming * unit, axis=0, keepdims=True)
    for j in range(8):
        at = slice(j * BLOCK, (j + 1) * BLOCK)
        for r in range(ROWS - 1):
            block[r * 8 + j : r * 8 + j + 1, :] = rows[r : r + 1, at]
        block[(ROWS - 1) * 8 + j : (ROWS - 1) * 8 + j + 1, :] = row[:, at]
    for i in range(spread.shape[0]):
        spread[i] = block[...].astype(spread.dtype)


def copy_kernel(*refs):
    count = len(refs) // 2
    for source, target in zip(refs[:count], refs[count:]):
        target[...] = source[...]


def tick_kernel(out):
    out[...] = jnp.zeros(out.shape, f32)


def hops(x, count):
    def tick(after):
        return call(tick_kernel, "tick", [((8, BLOCK), f32)], [], after=[after])[0]

    small = tick(x)
    for _ in range(count):
        small = tick(swap(small, CORE))
    return small


def merge_kernel(terms, outs):
    total = terms[0][...].astype(f32)
    for term in terms[1:]:
        total = total + term[...].astype(f32)
    at = 0
    for out in outs:
        out[...] = total[:, at : at + out.shape[1]].astype(out.dtype)
        at += out.shape[1]


def merge(terms, outs, after=()):
    count = len(terms)
    return call(
        lambda *refs: merge_kernel(refs[:count], refs[count:]),
        "merge",
        [((terms[0].shape[0], width), dtype) for width, dtype in outs],
        terms,
        after=after,
    )


def split_rows_kernel(terms, outs):
    near = lax.axis_index(NEAR)
    rows = outs[0].shape[0]
    for out, whose in zip(outs, (near, 1 - near)):
        here = pl.ds(pl.multiple_of(whose * rows, rows), rows)
        total = terms[0][here, :].astype(f32)
        for term in terms[1:]:
            total = total + term[here, :].astype(f32)
        out[...] = total.astype(out.dtype)


def totals_kernel(rows, power, sums):
    count = rows.shape[0]
    ids = rows[:, 4 * 8, 0:1].astype(f32).astype(jnp.int32)
    lane = lax.broadcasted_iota(jnp.int32, (count, SPEAKERS), 1)
    one_hot = (lane == ids).astype(f32)

    def per_speaker(x):
        return lax.dot_general(
            one_hot, x, (((0,), (0,)), ((), ())), precision=highest, preferred_element_type=f32
        )

    frames = per_speaker(jnp.full((count, BLOCK), float(BLOCK), f32))
    share = 1.0 / jnp.maximum(frames, 1.0)
    for j in range(8):
        power[:, j * BLOCK : (j + 1) * BLOCK] = per_speaker(rows[:, j, :].astype(f32)) * share
    total = rows[0].astype(f32)
    for i in range(1, count):
        total = total + rows[i].astype(f32)
    sums[...] = total


def kernel_pieces(pieces):
    if len(pieces) == PIECES:
        return pieces
    ordered = from_pieces(jnp.concatenate(pieces, axis=0), 0)
    size = ordered.shape[0] // PIECES
    split = [ordered[b * size : (b + 1) * size] for b in range(PIECES)]
    return [split[(j % 4) * 2 + j // 4] for j in range(PIECES)]


def far_order(x):
    count = far_count()
    far = lax.axis_index(FAR)
    size = x.shape[0] // count
    return jnp.concatenate(
        [lax.dynamic_slice_in_dim(x, (far ^ k) * size, size, 0) for k in range(count)], axis=0
    )


def line_pieces(pieces):
    if len(pieces) == LINE:
        return pieces
    return jnp.split(far_order(jnp.concatenate(pieces, axis=0)), LINE, axis=0)


def slice_weights(sources, halves=1):
    rows = sources[0][0].shape[0]
    parts = []
    for x, count in sources:
        width = x.shape[1] // (4 * count * halves)
        parts.append(
            x.reshape(rows, count, 4, halves, width)
            .transpose(2, 0, 3, 1, 4)
            .reshape(4, rows, halves, count * width)
        )
    joined = jnp.concatenate(parts, axis=3)
    return joined.reshape(4, rows, halves * joined.shape[3])


def quarter_columns(x):
    near, pair = lax.axis_index(NEAR), lax.axis_index(PAIR)
    both = (NEAR, PAIR)
    across = [(i, 3 - i) for i in range(4)]

    def part(i, k):
        rows = lax.dynamic_index_in_dim(x, pair ^ i, 0, keepdims=False)
        return lax.dynamic_slice_in_dim(rows, (near ^ k) * (rows.shape[1] // 2), rows.shape[1] // 2, 1)

    came = {
        (0, 0): part(0, 0),
        (0, 1): swap(part(0, 1), NEAR),
        (1, 0): swap(part(1, 0), PAIR),
        (1, 1): lax.ppermute(part(1, 1), both, across),
    }
    by_near = [
        (jnp.where(near == 0, came[i, 0], came[i, 1]), jnp.where(near == 0, came[i, 1], came[i, 0]))
        for i in range(2)
    ]
    out = []
    for k in range(2):
        out.append(jnp.where(pair == 0, by_near[0][k], by_near[1][k]))
        out.append(jnp.where(pair == 0, by_near[1][k], by_near[0][k]))
    return jnp.concatenate(out, axis=0)


def sum_wide(own, other, outs, after=()):
    if far_count() != LINE:
        return sum_wide_long(own, other, outs), []
    whole = [(own[0].shape[1], bf16)]
    near = [swap(x, NEAR) for x in other]
    third = merge([own[3], near[3]], whole, after)
    halfway = merge([own[2], near[2], swap_far(third[0], 1)], whole)[0]
    first = merge([own[1], near[1]], whole, third)[0]
    return merge([own[0], near[0], swap_far(first, 1), swap_far(halfway, 2)], outs), [first]


def sum_wide_long(own, other, outs):
    count = far_count()
    ordered = [(own + other)[(b % 2) * 4 + b // 2] for b in range(PIECES)]
    pieces = to_pieces(jnp.concatenate([x.astype(f32) for x in ordered], axis=0), 0)
    size = pieces.shape[0] // (2 * count)
    parts = {}
    for i in range(2):
        for k in range(count):
            at = (i * count + k) * size
            parts[i, k] = pieces[at : at + size]
    total = scatter_parts(parts)
    at = 0
    result = []
    for width, dtype in outs:
        result.append(total[:, at : at + width].astype(dtype))
        at += width
    return result


def split_rows(terms, after):
    rows, width = terms[0].shape
    if rows % 32 != 0:
        near = lax.axis_index(NEAR)
        total = sum(x.astype(f32) for x in terms).reshape(2, rows // 2, width)
        return (
            lax.dynamic_index_in_dim(total, near, 0, keepdims=False),
            lax.dynamic_index_in_dim(total, 1 - near, 0, keepdims=False).astype(bf16),
        )
    return call(
        lambda *refs: split_rows_kernel(refs[: len(terms)], refs[len(terms) :]),
        "merge",
        [((rows // 2, width), f32), ((rows // 2, width), bf16)],
        terms,
        after=after,
    )


def sum_line(parts):
    count = far_count()
    pieces = jnp.split(far_order(jnp.concatenate(parts, axis=0).astype(f32)), count, axis=0)
    for j in range(count - 1, 0, -1):
        low = j & -j
        pieces[j ^ low] = pieces[j ^ low] + swap_far(pieces[j].astype(bf16), low).astype(f32)
    return pieces[0]


def body(
    frames,
    out_grad,
    qkv_weight,
    out_weight,
    gate_up_weight,
    down_weight_t,
    norm_gain_one,
    norm_gain_two,
    layer_scale_one,
    layer_scale_two,
    speaker,
    clip_bounds,
):
    streams, shard_len, width = frames.shape
    pair = lax.axis_index(PAIR)
    core = lax.axis_index(CORE)
    near = lax.axis_index(NEAR)
    shard = pair * 2 + core
    group = width // 4
    hidden = gate_up_weight.shape[1] // 16
    head_size = width // HEADS
    tokens = 4 * shard_len

    slice_a = pair_columns(core_columns(slice_weights([(qkv_weight, 3), (out_weight, 1)])))
    slice_b = quarter_columns(core_columns(slice_weights([(gate_up_weight, 2), (down_weight_t, 1)], halves=2)))
    pieces_a = kernel_pieces(gather_rows(slice_a))
    line_b = gather_line(slice_b)
    pieces_b = line_pieces(line_b)

    bounds = clip_bounds.astype(jnp.int32)
    gain_one = norm_gain_one[None]
    gain_two = norm_gain_two[None]
    scale_one = layer_scale_one[None]
    scale_two = layer_scale_two[None]
    frames_here, grad_here = call(
        copy_kernel,
        "fence",
        [((shard_len, width), bf16)] * 2,
        [frames.reshape(shard_len, width), out_grad.reshape(shard_len, width)],
        after=[slice_a],
    )

    def spread(x):
        across = swap(x, PAIR)
        return x, swap(x, CORE), across, swap(across, CORE)

    frames_all = spread(frames_here)
    grad_all = (*spread(grad_here), *spread(swap(grad_here, NEAR)))

    block = shard ^ jnp.arange(4, dtype=jnp.int32)
    positions = (block[:, None] * shard_len + jnp.arange(shard_len, dtype=jnp.int32)[None]).reshape(-1)
    half_size = head_size // 2
    lane = jnp.arange(BLOCK, dtype=jnp.int32)
    inverse_freq = jnp.exp((lane % half_size).astype(f32) * (-math.log(10000.0) / half_size))
    angles = positions.astype(f32)[:, None] * inverse_freq[None, :]
    cosine = jnp.cos(angles)
    sine = jnp.where(lane % head_size < half_size, -1.0, 1.0)[None, :] * jnp.sin(angles)

    (out_own,) = call(
        out_kernel,
        "out",
        [((width, group), bf16)],
        pieces_a,
        [pltpu.SemaphoreType.DMA((PIECES,))],
        anywhere=range(PIECES),
    )
    normed_one, qkv, stat, att, att_to_core, att_to_pair = call(
        attend_kernel,
        "attend",
        [
            ((tokens, width), bf16),
            ((tokens, 3 * group), bf16),
            ((tokens, BLOCK), f32),
            ((tokens, group), bf16),
            ((tokens, group), bf16),
            ((tokens, group), bf16),
        ],
        [bounds, *frames_all, *pieces_a, gain_one, cosine, sine],
        [pltpu.VMEM((width, 3 * group), bf16), pltpu.SemaphoreType.DMA((PIECES,))],
        smem=1,
        anywhere=range(5, 5 + PIECES),
        megabytes=52,
        after=[line_b[1], line_b[2], out_own],
    )
    att_pair = swap(att_to_pair, PAIR)
    att_core = swap(att_to_core, CORE)
    att_both = swap(att_pair, CORE)
    out_pair = swap(out_own, PAIR)
    outs = (out_own, swap(out_own, CORE), out_pair, swap(out_pair, CORE))

    normed_here, normed_even, attended, residual, branch_one = call(
        residual_kernel,
        "residual",
        [
            ((tokens, width), bf16),
            ((tokens // 2, width), bf16),
            ((tokens, width), bf16),
            ((shard_len, width), f32),
            ((shard_len, width), f32),
        ],
        [*frames_all, att, att_core, att_pair, att_both, *outs, scale_one, gain_two],
        [pltpu.VMEM((tokens, width), f32)],
        megabytes=36,
        after=[line_b[3], *grad_all],
    )

    near_even = swap(normed_even, NEAR)
    near_odd = swap(near_even, CORE)
    rows_b = width // LINE
    keep, send, keep_late, send_late, *grads_b = call(
        mlp_kernel,
        "mlp",
        [((tokens, width), bf16)] * 4 + [((rows_b, 3 * hidden), bf16)] * LINE,
        [normed_here, near_even, near_odd, *grad_all, *pieces_b, scale_two],
        [
            pltpu.VMEM((2 * tokens, width), bf16),
            pltpu.VMEM((2 * tokens, width), bf16),
            pltpu.VMEM((2 * tokens, hidden), bf16),
            pltpu.VMEM((2 * tokens, 2 * hidden), bf16),
            pltpu.VMEM((width, 3 * hidden), bf16),
            pltpu.SemaphoreType.DMA((LINE,)),
        ],
        anywhere=range(11, 11 + LINE),
        megabytes=36,
    )

    half_shape = ((2 * shard_len, width), bf16)
    own_shape = ((shard_len, width), bf16)

    got = swap(send, CORE)
    to_near = call(near_kernel, "onward", [half_shape], [keep, got])[0]
    got_near = swap(to_near, NEAR)
    got_late = swap(send_late, CORE)
    to_near_late = call(near_kernel, "onward", [half_shape], [keep_late, got_late], after=[to_near])[0]
    to_pair = call(pair_kernel, "onward", [own_shape], [keep, got, got_near], after=[to_near_late])[0]
    near_late = swap(to_near_late, NEAR)
    residual_grad, attn_grad, rows = call(
        middle_kernel,
        "middle",
        [((shard_len, width), f32), ((shard_len, width), bf16), ((8, width), f32)],
        [keep, got, got_near, swap(to_pair, PAIR), grad_here, residual, branch_one, scale_one, gain_two],
    )
    to_pair_late = call(
        pair_kernel, "onward", [own_shape], [keep_late, got_late, near_late], after=[attn_grad]
    )[0]
    met_late = (keep_late, got_late, near_late, swap(to_pair_late, PAIR))
    if far_count() == LINE:
        third_b, first_b = swap_far(grads_b[3], 1), swap_far(grads_b[1], 1)
        halfway_b = merge([grads_b[2], third_b], [(3 * hidden, bf16)], [attn_grad])[0]
        terms_b = [grads_b[0], first_b, swap_far(halfway_b, 2)]
    else:
        halfway_b = sum_line(grads_b)
        terms_b = [halfway_b]
    keep, send, *grads_a = call(
        attend_back_kernel,
        "attend_back",
        [((2 * shard_len, width), f32), ((2 * shard_len, width), bf16)]
        + [((BLOCK, 4 * group), bf16)] * PIECES,
        [bounds, *spread(attn_grad), qkv, stat, cosine, sine, *outs, *pieces_a, normed_one, attended],
        [
            pltpu.VMEM((tokens, 3 * group), bf16),
            pltpu.VMEM((width, 3 * group), bf16),
            pltpu.VMEM((tokens, width), bf16),
            pltpu.VMEM((tokens, group), bf16),
            pltpu.VMEM((tokens, tokens), bf16),
            pltpu.VMEM((tokens, tokens), bf16),
            pltpu.VMEM((4, group, group), bf16),
            pltpu.VMEM((tokens, width), bf16),
            pltpu.VMEM((tokens, width), bf16),
            pltpu.SemaphoreType.DMA((6 + PIECES,)),
        ],
        smem=1,
        anywhere=range(9, 15 + PIECES),
        after=[to_pair_late, halfway_b],
    )
    own_a, other_a = grads_a[:4], grads_a[4:]
    got = swap(send, CORE)
    onward = call(onward_kernel, "onward", [((shard_len, width), bf16)], [keep, got])[0]
    output, rows = call(
        finish_kernel,
        "finish",
        [((shard_len, width), bf16), ((8, width), f32)],
        [speaker.astype(jnp.int32), *met_late, grad_here, residual, rows, scale_two],
        smem=1,
    )
    (query_sum, key_sum, value_sum, out_sum), passed_a = sum_wide(
        own_a, other_a, [(group, bf16)] * 3 + [(group, f32)]
    )
    kept_b, left_b = split_rows(terms_b, passed_a)
    came_b = swap(left_b, NEAR)
    frames_grad, shared = call(
        last_kernel,
        "last",
        [((shard_len, width), bf16), ((far_count() * 8, ROWS * 8, BLOCK), bf16)],
        [keep, got, swap(onward, PAIR), frames_here, residual_grad, gain_one, rows],
        [pltpu.VMEM((ROWS * 8, BLOCK), f32)],
    )
    speaker_power, sums = call(
        totals_kernel,
        "totals",
        [((SPEAKERS, width), f32), ((ROWS * 8, BLOCK), f32)],
        [lax.all_to_all(shared, ALL, 0, 0, tiled=True)],
    )
    sums = sums.reshape(ROWS, width)

    def near_order(kept, came):
        return jnp.concatenate(
            [jnp.where(near == 0, kept, came), jnp.where(near == 0, came, kept)], axis=1
        )

    kept_low = kept_b[:, : 2 * hidden].astype(bf16)
    gate_up_grad_out = place_gate_up(
        near_order(kept_low[:, :hidden], came_b[:, :hidden]),
        near_order(kept_low[:, hidden:], came_b[:, hidden : 2 * hidden]),
        pair,
        core,
    )
    down_grad = near_order(kept_b[:, 2 * hidden :], came_b[:, 2 * hidden :].astype(f32))
    qkv_grad_out = place_qkv(query_sum, key_sum, value_sum, pair, core)
    return (
        output.reshape(frames.shape),
        speaker_power,
        frames_grad.reshape(frames.shape),
        qkv_grad_out,
        out_sum,
        gate_up_grad_out,
        down_grad,
        sums[5],
        sums[2],
        sums[3],
        sums[1],
    )


def place_gate_up(gate, up, pair, core):
    narrow = (PAIR, CORE)
    shard = pair * 2 + core
    first = jnp.where(shard == 1, up, gate)
    second = jnp.where(shard == 0, up, gate)
    second = jnp.where(shard == 2, up, second)
    got_one = lax.ppermute(first, narrow, [(1, 2), (2, 1)])
    got_two = lax.ppermute(second, narrow, [(0, 2), (1, 0), (2, 3), (3, 1)])
    left = jnp.where(shard == 0, gate, jnp.where(shard == 1, got_one, got_two))
    right = jnp.where(shard == 3, up, jnp.where(shard == 2, got_one, got_two))
    return jnp.concatenate([left, right], axis=1).astype(f32)


def place_qkv(query, key, value, pair, core):
    shard = pair * 2 + core
    to_core = jnp.where(
        shard == 0, key, jnp.where(shard == 1, query, jnp.where(shard == 2, value, key))
    )
    to_pair = jnp.where(pair == 0, value, query)
    stay = jnp.where(shard == 0, query, jnp.where(shard == 3, value, key))
    got_core = swap(to_core, CORE)
    got_pair = swap(to_pair, PAIR)
    left = jnp.where(core == 0, stay, got_pair)
    right = jnp.where(core == 0, got_pair, stay)
    return jnp.concatenate([left, got_core, right], axis=1).astype(f32)


def solution(mesh):
    wide = mesh.shape["wide"]
    split = Mesh(mesh.devices.reshape(wide // 2, 2, 2, 2), ALL)
    both = (FAR, NEAR)
    narrow = (PAIR, CORE)
    placed = (
        P(both, narrow, None),
        P(both, narrow, None),
        P(ALL, None),
        P(ALL, None),
        P(ALL, None),
        P(ALL, None),
        P(),
        P(),
        P(),
        P(),
        P(both),
        P(both, None),
    )
    return jax.shard_map(
        body,
        mesh=split,
        in_specs=placed,
        out_specs=(
            P(both, narrow, None),
            P(),
            P(both, narrow, None),
            P(both, narrow),
            P(both, narrow),
            P(both, narrow),
            P(both, narrow),
            P(),
            P(),
            P(),
            P(),
        ),
        check_vma=False,
    )
```

```python
import functools
import math

import jax
import jax.numpy as jnp
from jax import lax
from jax.experimental import pallas as pl
from jax.experimental.pallas import tpu as pltpu
from jax.sharding import Mesh, PartitionSpec as P

HEADS = 16
WINDOW = 128
CLIP_LEN = 512
SPEAKERS = 128

bf16 = jnp.bfloat16
f32 = jnp.float32
highest = lax.Precision.HIGHEST

FAR, NEAR, PAIR, CORE = "far", "near", "pair", "core"
ALL = (FAR, NEAR, PAIR, CORE)
SWAP = [(0, 1), (1, 0)]


def swap(x, axis):
    return lax.ppermute(x, axis, SWAP)


def dot(a, b):
    return jnp.dot(a, b, preferred_element_type=f32)


def dot_t(a, b):
    return lax.dot_general(a, b, (((1,), (1,)), ((), ())), preferred_element_type=f32)


def tdot(a, b):
    return lax.dot_general(a, b, (((0,), (0,)), ((), ())), preferred_element_type=f32)


def far_count():
    return lax.axis_size(FAR)


def piece_index():
    far, near = lax.axis_index(FAR), lax.axis_index(NEAR)
    return [(far ^ k) * 2 + (near ^ i) for i in range(2) for k in range(far_count())]


def to_pieces(x, axis):
    size = x.shape[axis] // (2 * far_count())
    return jnp.concatenate(
        [lax.dynamic_slice_in_dim(x, i * size, size, axis) for i in piece_index()], axis=axis
    )


def from_pieces(x, axis):
    count = far_count()
    far, near = lax.axis_index(FAR), lax.axis_index(NEAR)
    size = x.shape[axis] // (2 * count)
    return jnp.concatenate(
        [
            lax.dynamic_slice_in_dim(x, ((near ^ i) * count + (far ^ k)) * size, size, axis)
            for k in range(count)
            for i in range(2)
        ],
        axis=axis,
    )


def swap_far(x, bit):
    return lax.ppermute(x, FAR, [(i, i ^ bit) for i in range(far_count())])


def gather_line(block):
    own = [block]
    for j in range(1, far_count()):
        low = j & -j
        own.append(swap_far(own[j ^ low], low))
    return own


def gather_rows(block):
    own = gather_line(block)
    return own + [swap(x, NEAR) for x in own]


def scatter_parts(parts):
    count = far_count()
    total = [
        parts[0, k] + swap(parts[1, k].astype(bf16), NEAR).astype(f32) for k in range(count)
    ]
    for j in range(count - 1, 0, -1):
        low = j & -j
        total[j ^ low] = total[j ^ low] + swap_far(total[j].astype(bf16), low).astype(f32)
    return total[0]


def core_columns(x):
    core = lax.axis_index(CORE)
    slices = [[x[0], x[1]], [x[2], x[3]]]
    stay = jnp.stack([jnp.where(core == 0, s[0], s[1]) for s in slices])
    send = jnp.stack([jnp.where(core == 0, s[1], s[0]) for s in slices])
    got = swap(send, CORE)
    return jnp.concatenate([jnp.where(core == 0, stay, got), jnp.where(core == 0, got, stay)], axis=1)


def pair_columns(x):
    pair = lax.axis_index(PAIR)
    stay = jnp.where(pair == 0, x[0], x[1])
    got = swap(jnp.where(pair == 0, x[1], x[0]), PAIR)
    return jnp.concatenate([jnp.where(pair == 0, stay, got), jnp.where(pair == 0, got, stay)], axis=0)


BLOCK = 128
PIECES = 8
LINE = 4
ROWS = 6
MICROSECONDS = dict(
    attend=9, residual=3, mlp=11, middle=2, finish=2, attend_back=11, last=2, rows=1, onward=1, merge=1, weight_grad=2,
    fence=1, tick=0, totals=1, out=0,
)
RATE = 10**8


def call(kernel, name, outs, ins, scratch=(), smem=0, anywhere=(), far_outs=(), megabytes=24, after=()):
    specs = []
    given = len(ins)
    if len(after) > 0:
        inner = kernel

        def kernel(*refs):
            inner(*refs[:given], *refs[given + len(after) :])

    for i in range(len(ins)):
        if i < smem:
            specs.append(pl.BlockSpec(memory_space=pltpu.SMEM))
        elif i in anywhere:
            specs.append(pl.BlockSpec(memory_space=pltpu.HBM))
        else:
            specs.append(pl.BlockSpec(memory_space=pltpu.VMEM))
    specs += [pl.BlockSpec(memory_space=pl.ANY)] * len(after)
    return pl.pallas_call(
        kernel,
        out_shape=[jax.ShapeDtypeStruct(shape, dtype) for shape, dtype in outs],
        in_specs=specs,
        out_specs=[
            pl.BlockSpec(memory_space=pltpu.HBM if i in far_outs else pltpu.VMEM) for i in range(len(outs))
        ],
        scratch_shapes=list(scratch),
        compiler_params=pltpu.CompilerParams(vmem_limit_bytes=megabytes * 2**20),
        cost_estimate=pl.CostEstimate(
            flops=int(MICROSECONDS[name] * RATE), bytes_accessed=0, transcendentals=0
        ),
        name=name,
    )(*ins, *after)


def wide_here():
    if lax.axis_size(FAR) != LINE:
        return 0
    return lax.axis_index(FAR) * 2 + lax.axis_index(NEAR)


def far_here():
    return lax.axis_index(FAR) if lax.axis_size(FAR) == LINE else 0


def shard_here():
    return lax.axis_index(PAIR) * 2 + lax.axis_index(CORE)


def feature_block(wide, piece):
    return wide ^ ((piece % 4) * 2 + piece // 4)


def lanes(block, size=BLOCK):
    return pl.ds(pl.multiple_of(block * size, size), size)


def normalise(x):
    centred = x - jnp.mean(x, axis=1, keepdims=True)
    inverse = lax.rsqrt(jnp.mean(centred * centred, axis=1, keepdims=True) + 1e-05)
    return centred * inverse, inverse


def turn(x, cos, sin, sign):
    lane = lax.broadcasted_iota(jnp.int32, x.shape, 1)
    lower = (lane & 63) < 32
    partner = jnp.where(lower, pltpu.roll(x, BLOCK - 32, 1), pltpu.roll(x, 32, 1))
    return x * cos + (sign * partner) * sin


def excluded(shard, block, first, second, keys):
    query = (shard ^ block) * BLOCK + lax.broadcasted_iota(jnp.int32, (BLOCK, 1), 0)
    lane = lax.broadcasted_iota(jnp.int32, (1, keys), 1)
    key = (shard ^ (lane // BLOCK)) * BLOCK + lane % BLOCK

    def segment(position):
        return (position >= first).astype(jnp.int32) + (position >= second).astype(jnp.int32)

    allowed = (jnp.abs(query - key) <= WINDOW) & (segment(query) == segment(key))
    return jnp.where(allowed, 0.0, -1e30)


def half_mask(head, shape):
    lane = lax.broadcasted_iota(jnp.int32, shape, 1)
    return (lane // 64) == head


def out_kernel(*refs):
    pieces, (out, sems) = refs[:PIECES], refs[PIECES:]
    group = out.shape[1]
    copies = [
        pltpu.make_async_copy(
            pieces[j].at[:, pl.ds(3 * group, group)],
            out.at[lanes(feature_block(wide_here(), j)), :],
            sems.at[j],
        )
        for j in range(PIECES)
    ]
    for copy in copies:
        copy.start()
    for copy in copies:
        copy.wait()


def attend_kernel(bounds, own, core, across, both, *refs):
    pieces = refs[:PIECES]
    gain, cos, sin, normed, qkv, stat, att, att_core, att_pair, weight, sems = refs[PIECES:]
    wide, shard, first, second = wide_here(), shard_here(), bounds[0, 0], bounds[0, 1]
    group = att.shape[1]
    copies = [
        pltpu.make_async_copy(
            pieces[j].at[:, pl.ds(0, 3 * group)], weight.at[lanes(feature_block(wide, j)), :], sems.at[j]
        )
        for j in range(PIECES)
    ]
    for copy in copies:
        copy.start()
    for b, x in enumerate((own, core, across, both)):
        unit, _ = normalise(x[...].astype(f32))
        normed[b * BLOCK : (b + 1) * BLOCK, :] = (unit * gain[...]).astype(bf16)
    for copy in copies:
        copy.wait()
    tiles = group // BLOCK
    for part in range(3):
        x = dot(normed[...], weight[:, part * group : (part + 1) * group])
        for t in range(tiles):
            y = x[:, t * BLOCK : (t + 1) * BLOCK]
            if part < 2:
                y = turn(y, cos[...], sin[...], 1.0)
            at = part * group + t * BLOCK
            qkv[:, at : at + BLOCK] = y.astype(bf16)
    keys = normed.shape[0]
    scale = 64**-0.5
    for b in range(4):
        here = slice(b * BLOCK, (b + 1) * BLOCK)
        bias = excluded(shard, b, first, second, keys)
        stats = jnp.zeros((BLOCK, BLOCK), f32)
        for t in range(tiles):
            query = qkv[here, t * BLOCK : (t + 1) * BLOCK] * jnp.bfloat16(scale)
            key = qkv[:, group + t * BLOCK : group + (t + 1) * BLOCK]
            value = qkv[:, 2 * group + t * BLOCK : 2 * group + (t + 1) * BLOCK]
            merged = None
            for h in range(2):
                keep = half_mask(h, query.shape)
                scores = dot_t(jnp.where(keep, query, jnp.zeros_like(query)), key) + bias
                peak = jnp.max(scores, axis=1, keepdims=True)
                exponent = jnp.exp(scores - peak)
                total = jnp.sum(exponent, axis=1, keepdims=True)
                probs = (exponent * (1.0 / total)).astype(bf16)
                lane = lax.broadcasted_iota(jnp.int32, stats.shape, 1)
                stats = jnp.where(lane == 2 * t + h, peak + jnp.log(total), stats)
                part = dot(probs, value)
                merged = part if merged is None else jnp.where(keep, part, merged)
            merged = merged.astype(bf16)
            cols = slice(t * BLOCK, (t + 1) * BLOCK)
            att[here, cols] = merged
            to_core, to_pair = b ^ 1, b ^ 2
            att_core[to_core * BLOCK : (to_core + 1) * BLOCK, cols] = merged
            att_pair[to_pair * BLOCK : (to_pair + 1) * BLOCK, cols] = merged
        stat[here, :] = stats


def residual_kernel(
    own, core, across, both, att0, att1, att2, att3, out0, out1, out2, out3, scale_one, gain_two,
    normed, normed_even, attended, residual_own, branch_own, branch,
):
    shard = shard_here()
    group = out0.shape[1]
    for m, part in enumerate((att0, att1)):
        attended[:, lanes(shard ^ m, group)] = part[...]
    attended[:, lanes(shard ^ 2, group)] = att2[...]
    for b in range(4):
        attended[b * BLOCK : (b + 1) * BLOCK, lanes(shard ^ 3, group)] = att3[
            (b ^ 1) * BLOCK : ((b ^ 1) + 1) * BLOCK, :
        ]
    for m, part in enumerate((out0, out1, out2, out3)):
        branch[:, lanes(shard ^ m, group)] = dot(attended[...], part[...])
    for b, x in enumerate((own, core, across, both)):
        here = slice(b * BLOCK, (b + 1) * BLOCK)
        total = x[...].astype(f32) + scale_one[...] * branch[here, :]
        unit, _ = normalise(total)
        low = (unit * gain_two[...]).astype(bf16)
        normed[here, :] = low
        if b % 2 == 0:
            normed_even[b // 2 * BLOCK : (b // 2 + 1) * BLOCK, :] = low
        if b == 0:
            residual_own[...] = total
            branch_own[...] = branch[here, :]


def mlp_kernel(normed_here, near_even, near_odd, *refs):
    grads, refs = refs[:8], refs[8:]
    pieces, scale_two, refs = refs[:LINE], refs[LINE], refs[LINE + 1 :]
    (keep, send, keep_late, send_late), outs, refs = refs[:4], refs[4 : 4 + LINE], refs[4 + LINE :]
    normed, mlp_grad, activated, gate_up_grad, weight, sems = refs
    far = far_here()
    rows = pieces[0].shape[0]
    copies = [
        pltpu.make_async_copy(pieces[k], weight.at[lanes(far ^ k, rows), :], sems.at[k]) for k in range(LINE)
    ]
    for copy in copies:
        copy.start()
    tokens = 4 * BLOCK
    normed[:tokens, :] = normed_here[...]
    for b in range(4):
        source = near_odd if b % 2 else near_even
        normed[tokens + b * BLOCK : tokens + (b + 1) * BLOCK, :] = source[b // 2 * BLOCK : (b // 2 + 1) * BLOCK, :]
    for b, x in enumerate(grads):
        mlp_grad[b * BLOCK : (b + 1) * BLOCK, :] = (scale_two[...] * x[...].astype(f32)).astype(bf16)
    for copy in copies:
        copy.wait()
    hidden = activated.shape[1]
    gate_at, up_at, down_at = [slice(i * hidden, (i + 1) * hidden) for i in range(3)]
    for stream in range(2):
        here = slice(stream * tokens, (stream + 1) * tokens)
        gate = dot(normed[here, :], weight[:, gate_at])
        up = dot(normed[here, :], weight[:, up_at])
        act_grad = dot(mlp_grad[here, :], weight[:, down_at])
        sigmoid = 1.0 / (1.0 + jnp.exp(-gate))
        silu = gate * sigmoid
        activated[here, :] = (silu * up).astype(bf16)
        gate_up_grad[here, gate_at] = (act_grad * up * sigmoid * (1.0 + gate * (1.0 - sigmoid))).astype(bf16)
        gate_up_grad[here, up_at] = (act_grad * silu).astype(bf16)
        back = dot_t(gate_up_grad[here, gate_at], weight[:, gate_at])
        back = (back + dot_t(gate_up_grad[here, up_at], weight[:, up_at])).astype(bf16)
        branch = dot_t(activated[here, :], weight[:, down_at]).astype(bf16)
        for b in range(4):
            here = slice(b * BLOCK, (b + 1) * BLOCK)
            at = stream * 2 * BLOCK + b // 2 * BLOCK
            early, late = (send, send_late) if b % 2 else (keep, keep_late)
            early[at : at + BLOCK, :] = back[here, :]
            late[at : at + BLOCK, :] = branch[here, :]
    for k, out in enumerate(outs):
        cols = lanes(far ^ k, rows)
        out[:, : 2 * hidden] = tdot(normed[:, cols], gate_up_grad[...]).astype(bf16)
        out[:, 2 * hidden :] = tdot(mlp_grad[:, cols], activated[...]).astype(bf16)


def near_kernel(keep, got, out):
    half = 2 * BLOCK
    out[...] = (keep[half:, :].astype(f32) + got[half:, :].astype(f32)).astype(bf16)


def pair_kernel(keep, got, got_near, out):
    at = slice(BLOCK, 2 * BLOCK)
    out[...] = (keep[at, :].astype(f32) + got[at, :].astype(f32) + got_near[at, :].astype(f32)).astype(bf16)


def own_sum(keep, got, got_near, got_pair):
    terms = (got, got_near, got_pair)
    total = keep[:BLOCK, :].astype(f32)
    for term in terms:
        total = total + term[:BLOCK, :].astype(f32)
    return total


def middle_kernel(
    keep, got, got_near, got_pair, own_grad, residual, branch_one, scale_one, gain_two,
    residual_grad, attn_grad, rows,
):
    incoming = own_sum(keep, got, got_near, got_pair)
    grad = own_grad[...].astype(f32)
    unit, inverse = normalise(residual[...])
    scaled = incoming * gain_two[...]
    back = inverse * (
        scaled
        - jnp.mean(scaled, axis=1, keepdims=True)
        - unit * jnp.mean(scaled * unit, axis=1, keepdims=True)
    )
    total = grad + back
    residual_grad[...] = total
    attn_grad[...] = (scale_one[...] * total).astype(bf16)
    rows[...] = jnp.zeros(rows.shape, f32)
    rows[2:3, :] = jnp.sum(incoming * unit, axis=0, keepdims=True)
    rows[3:4, :] = jnp.sum(total * branch_one[...], axis=0, keepdims=True)


def finish_kernel(speaker, keep, got, got_near, got_pair, own_grad, residual, rows_in, scale_two, output, rows):
    branch_two = own_sum(keep, got, got_near, got_pair)
    result = residual[...] + scale_two[...] * branch_two
    output[...] = result.astype(bf16)
    rows[0:1, :] = jnp.sum(result * result, axis=0, keepdims=True)
    rows[1:2, :] = jnp.sum(own_grad[...].astype(f32) * branch_two, axis=0, keepdims=True)
    rows[2:4, :] = rows_in[2:4, :]
    rows[4:5, :] = jnp.full((1, residual.shape[1]), speaker[0], jnp.int32).astype(f32)
    rows[5:8, :] = jnp.zeros((3, residual.shape[1]), f32)


def attend_back_kernel(bounds, own, core, across, both, qkv, stat, cos, sin, *refs):
    outs, pieces, lefts, refs = refs[:4], refs[4 : 4 + PIECES], refs[4 + PIECES : 6 + PIECES], refs[6 + PIECES :]
    shares, products, refs = refs[:4], refs[4 : 4 + PIECES], refs[4 + PIECES :]
    projected, weight, grads, att_grad, probs_all, score_all, biases, parts, normed, attended, sems = refs
    wide, shard, first, second = wide_here(), shard_here(), bounds[0, 0], bounds[0, 1]
    group = parts.shape[2]
    out_copies = [
        pltpu.make_async_copy(outs[m].at[lanes(shard, group), :], parts.at[m], sems.at[m]) for m in range(4)
    ]
    copies = [
        pltpu.make_async_copy(
            pieces[j].at[:, pl.ds(0, 3 * group)], weight.at[lanes(feature_block(wide, j)), :], sems.at[4 + j]
        )
        for j in range(PIECES)
    ]
    copies += [
        pltpu.make_async_copy(left, here, sems.at[4 + PIECES + i])
        for i, (left, here) in enumerate(zip(lefts, (normed, attended)))
    ]
    for copy in out_copies + copies:
        copy.start()
    for b, x in enumerate((own, core, across, both)):
        grads[b * BLOCK : (b + 1) * BLOCK, :] = x[...]
    for copy in out_copies:
        copy.wait()
    tiles = group // BLOCK
    total = None
    for m in range(4):
        product = dot_t(grads[:, lanes(shard ^ m, group)], parts[m])
        total = product if total is None else total + product
    att_grad[...] = total.astype(bf16)
    keys = qkv.shape[0]
    scale = 64**-0.5
    for b in range(4):
        biases[b * BLOCK : (b + 1) * BLOCK, :] = excluded(shard, b, first, second, keys)
    for t in range(tiles):
        cols = slice(t * BLOCK, (t + 1) * BLOCK)
        key = qkv[:, group + t * BLOCK : group + (t + 1) * BLOCK]
        value = qkv[:, 2 * group + t * BLOCK : 2 * group + (t + 1) * BLOCK]
        query_grad = [None] * 4
        key_grad = None
        value_grad = None
        for h in range(2):
            for b in range(4):
                here = slice(b * BLOCK, (b + 1) * BLOCK)
                query = qkv[here, cols] * jnp.bfloat16(scale)
                grad = att_grad[here, cols]
                keep_lanes = half_mask(h, query.shape)
                none = jnp.zeros_like(query)
                scores = dot_t(jnp.where(keep_lanes, query, none), key) + biases[here, :]
                probs = jnp.exp(scores - stat[here, 2 * t + h : 2 * t + h + 1])
                grad_here = jnp.where(keep_lanes, grad, none)
                prob_grad = dot_t(grad_here, value)
                delta = jnp.sum(probs * prob_grad, axis=1, keepdims=True)
                score_grad = (probs * (prob_grad - delta)).astype(bf16)
                probs_all[here, :] = probs.astype(bf16)
                score_all[here, :] = score_grad
                part = dot(score_grad, key)
                query_grad[b] = part if h == 0 else jnp.where(keep_lanes, part, query_grad[b])
            k_part = tdot(score_all[...], qkv[:, cols])
            v_part = tdot(probs_all[...], att_grad[:, cols])
            keep_all = half_mask(h, k_part.shape)
            key_grad = k_part if h == 0 else jnp.where(keep_all, k_part, key_grad)
            value_grad = v_part if h == 0 else jnp.where(keep_all, v_part, value_grad)
        for b in range(4):
            here = slice(b * BLOCK, (b + 1) * BLOCK)
            projected[here, cols] = turn(
                query_grad[b] * scale, cos[here, :], sin[here, :], -1.0
            ).astype(bf16)
        projected[:, group + t * BLOCK : group + (t + 1) * BLOCK] = turn(
            key_grad * scale, cos[...], sin[...], -1.0
        ).astype(bf16)
        projected[:, 2 * group + t * BLOCK : 2 * group + (t + 1) * BLOCK] = value_grad.astype(bf16)
    for copy in copies:
        copy.wait()
    for b, target in enumerate(shares):
        target[...] = dot_t(projected[b * BLOCK : (b + 1) * BLOCK, :], weight[...]).astype(target.dtype)
    for j, out in enumerate(products):
        cols = lanes(feature_block(wide, j))
        out[:, : 3 * group] = tdot(normed[:, cols], projected[...]).astype(bf16)
        out[:, 3 * group :] = tdot(attended[:, cols], grads[:, lanes(shard, group)]).astype(bf16)


def last_kernel(
    own, got_core, got_pair, got_both, frames, residual_grad, gain_one, rows, frames_grad, spread, block
):
    incoming = own[...]
    for term in (got_core, got_pair, got_both):
        incoming = incoming + term[...].astype(f32)
    unit, inverse = normalise(frames[...].astype(f32))
    scaled = incoming * gain_one[...]
    back = inverse * (
        scaled
        - jnp.mean(scaled, axis=1, keepdims=True)
        - unit * jnp.mean(scaled * unit, axis=1, keepdims=True)
    )
    frames_grad[...] = (residual_grad[...] + back).astype(bf16)
    row = jnp.sum(incoming * unit, axis=0, keepdims=True)
    for j in range(8):
        at = slice(j * BLOCK, (j + 1) * BLOCK)
        for r in range(ROWS - 1):
            block[r * 8 + j : r * 8 + j + 1, :] = rows[r : r + 1, at]
        block[(ROWS - 1) * 8 + j : (ROWS - 1) * 8 + j + 1, :] = row[:, at]
    for i in range(spread.shape[0]):
        spread[i] = block[...].astype(spread.dtype)


def copy_kernel(*refs):
    count = len(refs) // 2
    for source, target in zip(refs[:count], refs[count:]):
        target[...] = source[...]


def tick_kernel(out):
    out[...] = jnp.zeros(out.shape, f32)


def hops(x, count):
    def tick(after):
        return call(tick_kernel, "tick", [((8, BLOCK), f32)], [], after=[after])[0]

    small = tick(x)
    for _ in range(count):
        small = tick(swap(small, CORE))
    return small


def merge_kernel(terms, outs):
    total = terms[0][...].astype(f32)
    for term in terms[1:]:
        total = total + term[...].astype(f32)
    at = 0
    for out in outs:
        out[...] = total[:, at : at + out.shape[1]].astype(out.dtype)
        at += out.shape[1]


def merge(terms, outs, after=()):
    count = len(terms)
    return call(
        lambda *refs: merge_kernel(refs[:count], refs[count:]),
        "merge",
        [((terms[0].shape[0], width), dtype) for width, dtype in outs],
        terms,
        after=after,
    )


def split_rows_kernel(terms, outs):
    near = lax.axis_index(NEAR)
    rows = outs[0].shape[0]
    for out, whose in zip(outs, (near, 1 - near)):
        here = pl.ds(pl.multiple_of(whose * rows, rows), rows)
        total = terms[0][here, :].astype(f32)
        for term in terms[1:]:
            total = total + term[here, :].astype(f32)
        out[...] = total.astype(out.dtype)


def totals_kernel(rows, power, sums):
    count = rows.shape[0]
    ids = rows[:, 4 * 8, 0:1].astype(f32).astype(jnp.int32)
    lane = lax.broadcasted_iota(jnp.int32, (count, SPEAKERS), 1)
    one_hot = (lane == ids).astype(f32)

    def per_speaker(x):
        return lax.dot_general(
            one_hot, x, (((0,), (0,)), ((), ())), precision=highest, preferred_element_type=f32
        )

    frames = per_speaker(jnp.full((count, BLOCK), float(BLOCK), f32))
    share = 1.0 / jnp.maximum(frames, 1.0)
    for j in range(8):
        power[:, j * BLOCK : (j + 1) * BLOCK] = per_speaker(rows[:, j, :].astype(f32)) * share
    total = rows[0].astype(f32)
    for i in range(1, count):
        total = total + rows[i].astype(f32)
    sums[...] = total


def kernel_pieces(pieces):
    if len(pieces) == PIECES:
        return pieces
    ordered = from_pieces(jnp.concatenate(pieces, axis=0), 0)
    size = ordered.shape[0] // PIECES
    split = [ordered[b * size : (b + 1) * size] for b in range(PIECES)]
    return [split[(j % 4) * 2 + j // 4] for j in range(PIECES)]


def far_order(x):
    count = far_count()
    far = lax.axis_index(FAR)
    size = x.shape[0] // count
    return jnp.concatenate(
        [lax.dynamic_slice_in_dim(x, (far ^ k) * size, size, 0) for k in range(count)], axis=0
    )


def line_pieces(pieces):
    if len(pieces) == LINE:
        return pieces
    return jnp.split(far_order(jnp.concatenate(pieces, axis=0)), LINE, axis=0)


def slice_weights(sources, halves=1):
    rows = sources[0][0].shape[0]
    parts = []
    for x, count in sources:
        width = x.shape[1] // (4 * count * halves)
        parts.append(
            x.reshape(rows, count, 4, halves, width)
            .transpose(2, 0, 3, 1, 4)
            .reshape(4, rows, halves, count * width)
        )
    joined = jnp.concatenate(parts, axis=3)
    return joined.reshape(4, rows, halves * joined.shape[3])


def quarter_columns(x):
    near, pair = lax.axis_index(NEAR), lax.axis_index(PAIR)
    both = (NEAR, PAIR)
    across = [(i, 3 - i) for i in range(4)]

    def part(i, k):
        rows = lax.dynamic_index_in_dim(x, pair ^ i, 0, keepdims=False)
        return lax.dynamic_slice_in_dim(rows, (near ^ k) * (rows.shape[1] // 2), rows.shape[1] // 2, 1)

    came = {
        (0, 0): part(0, 0),
        (0, 1): swap(part(0, 1), NEAR),
        (1, 0): swap(part(1, 0), PAIR),
        (1, 1): lax.ppermute(part(1, 1), both, across),
    }
    by_near = [
        (jnp.where(near == 0, came[i, 0], came[i, 1]), jnp.where(near == 0, came[i, 1], came[i, 0]))
        for i in range(2)
    ]
    out = []
    for k in range(2):
        out.append(jnp.where(pair == 0, by_near[0][k], by_near[1][k]))
        out.append(jnp.where(pair == 0, by_near[1][k], by_near[0][k]))
    return jnp.concatenate(out, axis=0)


def sum_wide(own, other, outs, after, between):
    if far_count() != LINE:
        return sum_wide_long(own, other, outs), between(())
    whole = [(own[0].shape[1], bf16)]
    near = [swap(x, NEAR) for x in other]
    third = merge([own[3], near[3]], whole, after[0])
    first = merge([own[1], near[1]], whole, third)[0]
    halfway = merge([own[2], near[2], swap_far(third[0], 1)], whole, after[1])[0]
    done = between([halfway])
    terms = [own[0], near[0], swap_far(first, 1), swap_far(halfway, 2)]
    return merge(terms, outs, (done[1], done[2])), done


def sum_wide_long(own, other, outs):
    count = far_count()
    ordered = [(own + other)[(b % 2) * 4 + b // 2] for b in range(PIECES)]
    pieces = to_pieces(jnp.concatenate([x.astype(f32) for x in ordered], axis=0), 0)
    size = pieces.shape[0] // (2 * count)
    parts = {}
    for i in range(2):
        for k in range(count):
            at = (i * count + k) * size
            parts[i, k] = pieces[at : at + size]
    total = scatter_parts(parts)
    at = 0
    result = []
    for width, dtype in outs:
        result.append(total[:, at : at + width].astype(dtype))
        at += width
    return result


def split_rows(terms, after):
    rows, width = terms[0].shape
    if rows % 32 != 0:
        near = lax.axis_index(NEAR)
        total = sum(x.astype(f32) for x in terms).reshape(2, rows // 2, width)
        return (
            lax.dynamic_index_in_dim(total, near, 0, keepdims=False),
            lax.dynamic_index_in_dim(total, 1 - near, 0, keepdims=False).astype(bf16),
        )
    return call(
        lambda *refs: split_rows_kernel(refs[: len(terms)], refs[len(terms) :]),
        "merge",
        [((rows // 2, width), f32), ((rows // 2, width), bf16)],
        terms,
        after=after,
    )


def sum_line(parts):
    count = far_count()
    pieces = jnp.split(far_order(jnp.concatenate(parts, axis=0).astype(f32)), count, axis=0)
    for j in range(count - 1, 0, -1):
        low = j & -j
        pieces[j ^ low] = pieces[j ^ low] + swap_far(pieces[j].astype(bf16), low).astype(f32)
    return pieces[0]


def body(
    frames,
    out_grad,
    qkv_weight,
    out_weight,
    gate_up_weight,
    down_weight_t,
    norm_gain_one,
    norm_gain_two,
    layer_scale_one,
    layer_scale_two,
    speaker,
    clip_bounds,
):
    streams, shard_len, width = frames.shape
    pair = lax.axis_index(PAIR)
    core = lax.axis_index(CORE)
    near = lax.axis_index(NEAR)
    shard = pair * 2 + core
    group = width // 4
    hidden = gate_up_weight.shape[1] // 16
    head_size = width // HEADS
    tokens = 4 * shard_len

    slice_a = pair_columns(core_columns(slice_weights([(qkv_weight, 3), (out_weight, 1)])))
    slice_b = quarter_columns(core_columns(slice_weights([(gate_up_weight, 2), (down_weight_t, 1)], halves=2)))
    pieces_a = kernel_pieces(gather_rows(slice_a))
    line_b = gather_line(slice_b)
    pieces_b = line_pieces(line_b)

    bounds = clip_bounds.astype(jnp.int32)
    gain_one = norm_gain_one[None]
    gain_two = norm_gain_two[None]
    scale_one = layer_scale_one[None]
    scale_two = layer_scale_two[None]
    block = shard ^ jnp.arange(4, dtype=jnp.int32)
    positions = (block[:, None] * shard_len + jnp.arange(shard_len, dtype=jnp.int32)[None]).reshape(-1)
    half_size = head_size // 2
    lane = jnp.arange(BLOCK, dtype=jnp.int32)
    inverse_freq = jnp.exp((lane % half_size).astype(f32) * (-math.log(10000.0) / half_size))
    angles = positions.astype(f32)[:, None] * inverse_freq[None, :]
    cosine = jnp.cos(angles)
    sine = jnp.where(lane % head_size < half_size, -1.0, 1.0)[None, :] * jnp.sin(angles)

    frames_here, grad_here = call(
        copy_kernel,
        "fence",
        [((shard_len, width), bf16)] * 2,
        [frames.reshape(shard_len, width), out_grad.reshape(shard_len, width)],
        after=[slice_a, cosine, sine],
    )

    def spread(x):
        across = swap(x, PAIR)
        return x, swap(x, CORE), across, swap(across, CORE)

    frames_all = spread(frames_here)
    grad_all = (*spread(grad_here), *spread(swap(grad_here, NEAR)))

    (out_own,) = call(
        out_kernel,
        "out",
        [((width, group), bf16)],
        pieces_a,
        [pltpu.SemaphoreType.DMA((PIECES,))],
        anywhere=range(PIECES),
    )
    normed_one, qkv, stat, att, att_to_core, att_to_pair = call(
        attend_kernel,
        "attend",
        [
            ((tokens, width), bf16),
            ((tokens, 3 * group), bf16),
            ((tokens, BLOCK), f32),
            ((tokens, group), bf16),
            ((tokens, group), bf16),
            ((tokens, group), bf16),
        ],
        [bounds, *frames_all, *pieces_a, gain_one, cosine, sine],
        [pltpu.VMEM((width, 3 * group), bf16), pltpu.SemaphoreType.DMA((PIECES,))],
        smem=1,
        anywhere=range(5, 5 + PIECES),
        megabytes=52,
        after=[out_own],
    )
    att_to_core, att_to_pair = call(copy_kernel, "fence", [((tokens, group), bf16)] * 2, [att_to_core, att_to_pair], after=[line_b[1], line_b[2]])
    att_pair = swap(att_to_pair, PAIR)
    att_core = swap(att_to_core, CORE)
    att_both = swap(att_pair, CORE)
    out_pair = swap(out_own, PAIR)
    outs = (out_own, swap(out_own, CORE), out_pair, swap(out_pair, CORE))

    normed_here, normed_even, attended, residual, branch_one = call(
        residual_kernel,
        "residual",
        [
            ((tokens, width), bf16),
            ((tokens // 2, width), bf16),
            ((tokens, width), bf16),
            ((shard_len, width), f32),
            ((shard_len, width), f32),
        ],
        [*frames_all, att, att_core, att_pair, att_both, *outs, scale_one, gain_two],
        [pltpu.VMEM((tokens, width), f32)],
        megabytes=36,
        after=[*grad_all],
    )

    near_even = swap(normed_even, NEAR)
    near_odd = swap(near_even, CORE)
    rows_b = width // LINE
    keep, send, keep_late, send_late, *grads_b = call(
        mlp_kernel,
        "mlp",
        [((tokens, width), bf16)] * 4 + [((rows_b, 3 * hidden), bf16)] * LINE,
        [normed_here, near_even, near_odd, *grad_all, *pieces_b, scale_two],
        [
            pltpu.VMEM((2 * tokens, width), bf16),
            pltpu.VMEM((2 * tokens, width), bf16),
            pltpu.VMEM((2 * tokens, hidden), bf16),
            pltpu.VMEM((2 * tokens, 2 * hidden), bf16),
            pltpu.VMEM((width, 3 * hidden), bf16),
            pltpu.SemaphoreType.DMA((LINE,)),
        ],
        anywhere=range(11, 11 + LINE),
        megabytes=36,
    )

    half_shape = ((2 * shard_len, width), bf16)
    own_shape = ((shard_len, width), bf16)

    got = swap(send, CORE)
    to_near = call(near_kernel, "onward", [half_shape], [keep, got])[0]
    got_near = swap(to_near, NEAR)
    got_late = swap(send_late, CORE)
    to_near_late = call(near_kernel, "onward", [half_shape], [keep_late, got_late], after=[to_near])[0]
    to_pair = call(pair_kernel, "onward", [own_shape], [keep, got, got_near], after=[to_near_late])[0]
    near_late = swap(to_near_late, NEAR)
    residual_grad, attn_grad, rows = call(
        middle_kernel,
        "middle",
        [((shard_len, width), f32), ((shard_len, width), bf16), ((8, width), f32)],
        [keep, got, got_near, swap(to_pair, PAIR), grad_here, residual, branch_one, scale_one, gain_two],
    )
    to_pair_late = call(
        pair_kernel, "onward", [own_shape], [keep_late, got_late, near_late], after=[attn_grad]
    )[0]
    met_late = (keep_late, got_late, near_late, swap(to_pair_late, PAIR))
    if far_count() == LINE:
        third_b, first_b = swap_far(grads_b[3], 1), swap_far(grads_b[1], 1)
        halfway_b = merge([grads_b[2], third_b], [(3 * hidden, bf16)], [attn_grad])[0]
        terms_b = [grads_b[0], first_b, swap_far(halfway_b, 2)]
    else:
        halfway_b = sum_line(grads_b)
        terms_b = [halfway_b]
    own_share, to_core, to_pair_share, to_both, *grads_a = call(
        attend_back_kernel,
        "attend_back",
        [((shard_len, width), f32)] + [((shard_len, width), bf16)] * 3
        + [((BLOCK, 4 * group), bf16)] * PIECES,
        [bounds, *spread(attn_grad), qkv, stat, cosine, sine, *outs, *pieces_a, normed_one, attended],
        [
            pltpu.VMEM((tokens, 3 * group), bf16),
            pltpu.VMEM((width, 3 * group), bf16),
            pltpu.VMEM((tokens, width), bf16),
            pltpu.VMEM((tokens, group), bf16),
            pltpu.VMEM((tokens, tokens), bf16),
            pltpu.VMEM((tokens, tokens), bf16),
            pltpu.VMEM((tokens, tokens), f32),
            pltpu.VMEM((4, group, group), bf16),
            pltpu.VMEM((tokens, width), bf16),
            pltpu.VMEM((tokens, width), bf16),
            pltpu.SemaphoreType.DMA((6 + PIECES,)),
        ],
        smem=1,
        anywhere=range(9, 15 + PIECES),
        after=[to_pair_late, halfway_b],
    )
    own_a, other_a = grads_a[:4], grads_a[4:]
    from_core = swap(to_core, CORE)
    from_pair = swap(to_pair_share, PAIR)
    from_both = lax.ppermute(to_both, (PAIR, CORE), [(i, 3 - i) for i in range(4)])
    output, rows = call(
        finish_kernel,
        "finish",
        [((shard_len, width), bf16), ((8, width), f32)],
        [speaker.astype(jnp.int32), *met_late, grad_here, residual, rows, scale_two],
        smem=1,
    )
    def meanwhile(ready):
        kept, left = split_rows(terms_b, ready)
        frames_grad, shared = call(
            last_kernel,
            "last",
            [((shard_len, width), bf16), ((far_count() * 8, ROWS * 8, BLOCK), bf16)],
            [own_share, from_core, from_pair, from_both, frames_here, residual_grad, gain_one, rows],
            [pltpu.VMEM((ROWS * 8, BLOCK), f32)],
            after=[left],
        )
        return kept, left, frames_grad, shared

    (query_sum, key_sum, value_sum, out_sum), (kept_b, left_b, frames_grad, shared) = sum_wide(
        own_a, other_a, [(group, bf16)] * 3 + [(group, f32)], ((), terms_b[1:], ()),
        meanwhile,
    )
    came_b = swap(left_b, NEAR)
    shared = lax.all_to_all(shared, ALL, 0, 0, tiled=True)
    speaker_power, sums = call(
        totals_kernel,
        "totals",
        [((SPEAKERS, width), f32), ((ROWS * 8, BLOCK), f32)],
        [shared],
        after=(),
    )
    sums = sums.reshape(ROWS, width)

    def near_order(kept, came):
        return jnp.concatenate(
            [jnp.where(near == 0, kept, came), jnp.where(near == 0, came, kept)], axis=1
        )

    kept_low = kept_b[:, : 2 * hidden].astype(bf16)
    gate_up_grad_out = place_gate_up(
        near_order(kept_low[:, :hidden], came_b[:, :hidden]),
        near_order(kept_low[:, hidden:], came_b[:, hidden : 2 * hidden]),
        pair,
        core,
    )
    down_grad = near_order(kept_b[:, 2 * hidden :], came_b[:, 2 * hidden :].astype(f32))
    qkv_grad_out = place_qkv(query_sum, key_sum, value_sum, pair, core)
    return (
        output.reshape(frames.shape),
        speaker_power,
        frames_grad.reshape(frames.shape),
        qkv_grad_out,
        out_sum,
        gate_up_grad_out,
        down_grad,
        sums[5],
        sums[2],
        sums[3],
        sums[1],
    )


def place_gate_up(gate, up, pair, core):
    narrow = (PAIR, CORE)
    shard = pair * 2 + core
    first = jnp.where(shard == 1, up, gate)
    second = jnp.where(shard == 0, up, gate)
    second = jnp.where(shard == 2, up, second)
    got_one = lax.ppermute(first, narrow, [(1, 2), (2, 1)])
    got_two = lax.ppermute(second, narrow, [(0, 2), (1, 0), (2, 3), (3, 1)])
    left = jnp.where(shard == 0, gate, jnp.where(shard == 1, got_one, got_two))
    right = jnp.where(shard == 3, up, jnp.where(shard == 2, got_one, got_two))
    return jnp.concatenate([left, right], axis=1).astype(f32)


def place_qkv(query, key, value, pair, core):
    shard = pair * 2 + core
    to_core = jnp.where(
        shard == 0, key, jnp.where(shard == 1, query, jnp.where(shard == 2, value, key))
    )
    to_pair = jnp.where(pair == 0, value, query)
    stay = jnp.where(shard == 0, query, jnp.where(shard == 3, value, key))
    got_core = swap(to_core, CORE)
    got_pair = swap(to_pair, PAIR)
    left = jnp.where(core == 0, stay, got_pair)
    right = jnp.where(core == 0, got_pair, stay)
    return jnp.concatenate([left, got_core, right], axis=1).astype(f32)


def solution(mesh):
    wide = mesh.shape["wide"]
    split = Mesh(mesh.devices.reshape(wide // 2, 2, 2, 2), ALL)
    both = (FAR, NEAR)
    narrow = (PAIR, CORE)
    placed = (
        P(both, narrow, None),
        P(both, narrow, None),
        P(ALL, None),
        P(ALL, None),
        P(ALL, None),
        P(ALL, None),
        P(),
        P(),
        P(),
        P(),
        P(both),
        P(both, None),
    )
    return jax.shard_map(
        body,
        mesh=split,
        in_specs=placed,
        out_specs=(
            P(both, narrow, None),
            P(),
            P(both, narrow, None),
            P(both, narrow),
            P(both, narrow),
            P(both, narrow),
            P(both, narrow),
            P(),
            P(),
            P(),
            P(),
        ),
        check_vma=False,
    )
```
